32 devices in a mesh: cube: 2 (over x), row: 4 (over y, core), col: 4 (over z).
Axes of the slice: x: 2, y: 2, z: 4, core: 2. Of those that a mesh axis runs over, the one named last changes fastest.
Arguments:
- child_update: float32 [8, 2, 16, 128, 128, 128], P(('cube', 'row'), None, None, None, 'col'), may hold values from -13 to 13
- child_map: int32 [2, 16384], replicated, may hold values from -1 to 16383, as said below
- parent_diag: float32 [16384], replicated, may hold values from 0.5 to 2
Outputs:
- updated: float32 [8, 16, 128, 128, 128], P(('cube', 'row'), None, None, 'col')
The draws below stay inside these ranges and needn't reach their ends.
Inputs may be any that keep to these rules, and one draw needn't show every extreme that they name: `child_map`: for each child and each aligned block of 128 child rows, the live rows (entries other than -1) come first and map, strictly increasing, into the same aligned block of 128 parent rows; every block has at least one -1 entry and uses the last parent row of its block.
All inputs are finite; a program needn't handle non-finite values.
Results may differ from the reference program's by a relative error of at most 0.0001.
Values sent between devices are 32-bit elements; how exact they have to be, the bound alone decides.
No kernel may reach another device: no remote copies, remote signals or barrier semaphores. Data moves between devices by JAX's collectives and lax.ppermute only.
A program may use at most 320 MiB of HBM per device.

```python
import math
import jax
import jax.numpy as jnp
from jax import lax

FRONT = 16384
K = 1024
TB = 128
RANKS = 512
GRID2 = 8
HALF = 4
TL = 16
CT = 128
CTL = 32
N_COL = 4


def draw_child_update(key, part):
    key_factor = jax.random.fold_in(jax.random.fold_in(key, 7), 0)
    factors = jax.random.normal(key_factor, (2, FRONT, RANKS), jnp.float32)
    gram = jnp.einsum('eik,ejk->eij', factors, factors, precision=lax.Precision.HIGHEST) / RANKS
    gram = gram.reshape(2, TL, 2, HALF, TB, FRONT)
    gram = jnp.transpose(gram, (0, 3, 2, 1, 4, 5)).reshape(GRID2, 2, TL, TB, FRONT)
    gram = gram.reshape(GRID2, 2, TL, TB, CTL, CT // CTL, TB)
    gram = jnp.swapaxes(gram, 4, 5)
    return gram.reshape(GRID2, 2, TL, TB, CT, TB)


def draw_child_map(key, part):
    key_count, key_order = jax.random.split(jax.random.fold_in(key, 11))
    counts = jax.random.randint(key_count, (2, CT), TB * 3 // 8, TB - TB // 16)
    offsets = jnp.arange(TB, dtype=jnp.int32)
    scores = jax.random.randint(key_order, (2, CT, TB), 0, 1 << 20) * TB + offsets
    ranks = jnp.argsort(jnp.argsort(scores, axis=-1), axis=-1).astype(jnp.int32)
    chosen = (ranks < counts[..., None] - 1) | (offsets == TB - 1)
    chosen_rank = jnp.cumsum(chosen.astype(jnp.int32), axis=-1) - 1
    live = jnp.sum(chosen.astype(jnp.int32), axis=-1)
    matches = chosen[..., None, :] & (chosen_rank[..., None, :] == offsets[:, None])
    slot_offset = jnp.sum(jnp.where(matches, offsets[None, :], 0), axis=-1).astype(jnp.int32)
    starts = (jnp.arange(CT, dtype=jnp.int32) * TB)[None, :, None]
    mapped = jnp.where(offsets < live[..., None], starts + slot_offset, -1)
    return mapped.reshape(2, FRONT).astype(jnp.int32)


def setup_inputs(seed: int = 0) -> dict:
    splits = jax.random.split(jax.random.key(seed), 4)
    child_update = draw_child_update(jax.random.fold_in(splits[3], 71), 0)
    child_map = draw_child_map(jax.random.fold_in(splits[3], 71), 0)
    parent_diag = jnp.clip(jnp.exp(jax.random.uniform(splits[2], (FRONT,), jnp.float32, math.log(0.5), math.log(2.0))), 0.5, 2.0)
    return {"child_update": child_update, "child_map": child_map, "parent_diag": parent_diag}


def natural_columns(stored):
    leading = stored.shape[:-2]
    grouped = stored.reshape(leading + (N_COL, CTL, TB))
    grouped = jnp.swapaxes(grouped, -3, -2)
    return grouped.reshape(leading + (FRONT,))

def tile_onehot(tile_map):
    blocks = tile_map.reshape(CT, TB)
    starts = (jnp.arange(CT, dtype=jnp.int32) * TB)[:, None, None]
    offsets = jnp.arange(TB, dtype=jnp.int32)[None, :, None]
    return (blocks[:, None, :] == starts + offsets).astype(jnp.float32)

def reference(child_update, child_map, parent_diag):
    children = child_update.reshape(2, HALF, 2, TL, TB, CT, TB)
    children = jnp.transpose(children, (0, 3, 2, 1, 4, 5, 6)).reshape(2, FRONT, CT, TB)
    children = natural_columns(children)
    front = jnp.diag(parent_diag)
    for sibling in range(2):
        onehot = tile_onehot(child_map[sibling])
        placed = jnp.einsum('tos,tsj->toj', onehot, children[sibling].reshape(CT, TB, FRONT), precision=lax.Precision.HIGHEST)
        placed = jnp.einsum('iuv,uov->iuo', placed.reshape(FRONT, CT, TB), onehot, precision=lax.Precision.HIGHEST)
        front = front + placed.reshape(FRONT, FRONT)
    factor = jnp.linalg.cholesky(front[:K, :K])
    panel = jax.scipy.linalg.solve_triangular(factor, front[:, :K].T, lower=True).T
    trailing = front[:, K:] - jnp.dot(panel.astype(jnp.float32), panel[K:].T.astype(jnp.float32), preferred_element_type=jnp.float32, precision=lax.Precision.HIGHEST)
    whole = jnp.concatenate([panel, trailing], axis=1)
    whole = jnp.transpose(whole.reshape(TL, GRID2, TB, FRONT), (1, 0, 2, 3))
    whole = whole.reshape(GRID2, TL, TB, CTL, N_COL, TB)
    whole = jnp.swapaxes(whole, 3, 4)
    return whole.reshape(GRID2, TL, TB, CT, TB)
```

```python
import jax
import jax.numpy as jnp
import numpy as np
from jax import lax
from jax.experimental import pallas as pl
from jax.experimental.pallas import tpu as pltpu
from jax.sharding import PartitionSpec as P

K = 1024
F32 = jnp.float32
BF16 = jnp.bfloat16
SUB = 8
VMEM_LIMIT = 56 * 1024 * 1024


def params(steps=1):
    return pltpu.CompilerParams(
        dimension_semantics=("arbitrary",) * steps, vmem_limit_bytes=VMEM_LIMIT
    )


def cost(flops, moved):
    return pl.CostEstimate(flops=int(flops), bytes_accessed=int(moved), transcendentals=0)


def swapped(value, axis, distance):
    mask = 2**distance
    pairs = [(source, source ^ mask) for source in range(lax.axis_size(axis))]
    return lax.ppermute(value, axis, pairs)


def after(value, *others):
    return lax.optimization_barrier((value,) + others)[0]


def inverse_map(values, starts):
    tile = values.shape[-1]
    offsets = jnp.arange(tile, dtype=jnp.int32)
    hit = (values - starts[:, None])[:, None, :] == offsets[None, :, None]
    return jnp.sum(jnp.where(hit, offsets[None, None, :] + 1, 0), axis=-1).astype(jnp.int32) - 1


def split(value):
    high = value.astype(BF16)
    return high, (value - high.astype(F32)).astype(BF16)


def dot(a, b):
    return jnp.dot(a, b, preferred_element_type=F32)


def dot_nt(a, b):
    return lax.dot_general(a, b, (((1,), (1,)), ((), ())), preferred_element_type=F32)


def dot_full(a, b, dims):
    return lax.dot_general(
        a, b, (dims, ((), ())), precision=lax.Precision.HIGHEST, preferred_element_type=F32
    )


def pack_panel(child, half, count):
    _, _, rows, tile, _, lanes = child.shape

    def kernel(half_ref, raw, out):
        for p in range(count):
            out[0, p] = raw.reshape(tile * SUB, lanes)[pl.ds(p, tile, SUB), :]

    return pl.pallas_call(
        kernel,
        grid_spec=pltpu.PrefetchScalarGridSpec(
            num_scalar_prefetch=1,
            grid=(rows,),
            in_specs=[
                pl.BlockSpec((1, 1, 1, tile, SUB, lanes), lambda j, h: (0, h[0], j, 0, 0, 0))
            ],
            out_specs=pl.BlockSpec((1, count, tile, lanes), lambda j, h: (j, 0, 0, 0)),
        ),
        out_shape=jax.ShapeDtypeStruct((rows, count, tile, lanes), F32),
        compiler_params=params(),
        cost_estimate=cost(0, rows * tile * lanes * 4 * (SUB + count)),
        name="pack_panel",
    )(half, child)


def pack_cross(child, half, parity):
    _, _, rows, tile, cols, lanes = child.shape
    pairs = cols // 2

    def kernel(half_ref, parity_ref, raw, out):
        for i in range(1, pairs):
            at = pl.ds(2 * i + parity_ref[0], tile, cols)
            out[0, i - 1] = raw.reshape(tile * cols, lanes)[at, :]

    return pl.pallas_call(
        kernel,
        grid_spec=pltpu.PrefetchScalarGridSpec(
            num_scalar_prefetch=2,
            grid=(rows - 1,),
            in_specs=[
                pl.BlockSpec(
                    (1, 1, 1, tile, cols, lanes), lambda j, h, b: (0, h[0], j + 1, 0, 0, 0)
                )
            ],
            out_specs=pl.BlockSpec((1, pairs - 1, tile, lanes), lambda j, h, b: (j, 0, 0, 0)),
        ),
        out_shape=jax.ShapeDtypeStruct((rows - 1, pairs - 1, tile, lanes), F32),
        compiler_params=params(),
        cost_estimate=cost(0, rows * tile * lanes * 4 * (cols + pairs)),
        name="pack_cross",
    )(half, parity, child)


def pack_lower(child, half, parity, first, last):
    _, _, _, tile, cols, lanes = child.shape
    base = first * (first - 1) // 2
    count = last * (last - 1) // 2 - base

    def kernel(half_ref, parity_ref, raw, out):
        j = pl.program_id(0) + first
        start = j * (j - 1) // 2 - base - 1
        for i in range(1, last):
            @pl.when(i <= j)
            def _():
                at = pl.ds(2 * i + parity_ref[0], tile, cols)
                out[start + i] = raw.reshape(tile * cols, lanes)[at, :]

    return pl.pallas_call(
        kernel,
        grid_spec=pltpu.PrefetchScalarGridSpec(
            num_scalar_prefetch=2,
            grid=(last - first,),
            in_specs=[
                pl.BlockSpec(
                    (1, 1, 1, tile, cols, lanes), lambda j, h, b: (0, h[0], j + first, 0, 0, 0)
                )
            ],
            out_specs=pl.BlockSpec((count, tile, lanes), lambda j, h, b: (0, 0, 0)),
        ),
        out_shape=jax.ShapeDtypeStruct((count, tile, lanes), F32),
        compiler_params=params(),
        cost_estimate=cost(0, tile * lanes * 4 * ((last - first) * cols + count)),
        name="pack_lower",
    )(half, parity, child)


def pack_all(child, half):
    _, _, rows, tile, cols, lanes = child.shape

    def kernel(half_ref, raw, out):
        for p in range(cols):
            out[0, p] = raw.reshape(tile * cols, lanes)[pl.ds(p, tile, cols), :]

    return pl.pallas_call(
        kernel,
        grid_spec=pltpu.PrefetchScalarGridSpec(
            num_scalar_prefetch=1,
            grid=(rows - 1,),
            in_specs=[
                pl.BlockSpec((1, 1, 1, tile, cols, lanes), lambda j, h: (0, h[0], j + 1, 0, 0, 0))
            ],
            out_specs=pl.BlockSpec((1, cols, tile, lanes), lambda j, h: (j, 0, 0, 0)),
        ),
        out_shape=jax.ShapeDtypeStruct((rows - 1, cols, tile, lanes), F32),
        compiler_params=params(),
        cost_estimate=cost(0, rows * tile * lanes * 8 * cols),
        name="pack_all",
    )(half, child)


def gathered_row(index, load, columns):
    row = load(jnp.maximum(index, 0))
    placed = jnp.take_along_axis(
        row, jnp.maximum(columns, 0), axis=1, mode="promise_in_bounds"
    )
    return jnp.where((columns >= 0) & (index >= 0), placed, 0.0)


def place_rows(first, second, maps, diag, where):
    count, tile, cols, lanes = first.shape
    (rows0, cols0), (rows1, cols1) = maps

    def kernel(rows0_ref, rows1_ref, where_ref, u0, u1, c0, c1, d, out):
        n, g = pl.program_id(0), pl.program_id(1)
        cols_0, cols_1 = c0[...], c1[...]

        def body(step, carry):
            for r in range(SUB):
                o = step * SUB + r
                value = gathered_row(rows0_ref[n, o], lambda s: u0[0, s], cols_0)
                value += gathered_row(rows1_ref[n, o], lambda s: u1[0, s], cols_1)
                for p in range(SUB):
                    out[0, p, pl.ds(o, 1), :] = value[p : p + 1, :]
            return carry

        lax.fori_loop(0, tile // SUB, body, 0)
        for p in range(SUB):
            @pl.when(where_ref[n] == g * SUB + p)
            def _():
                eye = lax.broadcasted_iota(jnp.int32, (tile, lanes), 0) == (
                    lax.broadcasted_iota(jnp.int32, (tile, lanes), 1)
                )
                out[0, p] += jnp.where(eye, d[0], 0.0)

    return pl.pallas_call(
        kernel,
        grid_spec=pltpu.PrefetchScalarGridSpec(
            num_scalar_prefetch=3,
            grid=(count, cols // SUB),
            in_specs=[
                pl.BlockSpec((1, tile, SUB, lanes), lambda n, g, *_: (n, 0, g, 0)),
                pl.BlockSpec((1, tile, SUB, lanes), lambda n, g, *_: (n, 0, g, 0)),
                pl.BlockSpec((SUB, lanes), lambda n, g, *_: (g, 0)),
                pl.BlockSpec((SUB, lanes), lambda n, g, *_: (g, 0)),
                pl.BlockSpec((1, 1, lanes), lambda n, g, *_: (n, 0, 0)),
            ],
            out_specs=pl.BlockSpec((1, SUB, tile, lanes), lambda n, g, *_: (n, g, 0, 0)),
        ),
        out_shape=jax.ShapeDtypeStruct((count, cols, tile, lanes), F32),
        compiler_params=params(2),
        cost_estimate=cost(0, count * cols * tile * lanes * 12),
        name="place_rows",
    )(rows0, rows1, where, first, second, cols0, cols1, diag[:, None, :])


def eliminate(block):
    tile = block.shape[0]
    lane = lax.broadcasted_iota(jnp.int32, (1, tile), 1)
    sub = lax.broadcasted_iota(jnp.int32, (tile, 1), 0)

    def body(j, carry):
        whole = block[...]
        row = block[pl.ds(j, 1), :]
        here = lane == j
        pivot = jnp.sum(jnp.where(here, row, 0.0), axis=1, keepdims=True)
        root = lax.rsqrt(pivot)
        root = root * (1.5 - 0.5 * pivot * root * root)
        row = jnp.where(here, root, row * root)
        column = jnp.sum(jnp.where(here, whole, 0.0), axis=1, keepdims=True) * root
        column = jnp.where(sub > j, column, 0.0)
        kept = jnp.where(here & (sub > j), 0.0, whole)
        block[...] = jnp.where(sub == j, row, kept - column * row)
        return carry

    lax.fori_loop(0, tile, body, 0)
    low = lax.broadcasted_iota(jnp.int32, (tile, tile), 0) >= (
        lax.broadcasted_iota(jnp.int32, (tile, tile), 1)
    )
    return jnp.where(low, block[...], 0.0)


def inverse_factor(pivot, tile):
    order = pivot.shape[0]
    steps = order // tile

    def kernel(a, high, low, m, block):
        m[...] = a[...]
        for s in range(steps):
            top, end = s * tile, (s + 1) * tile
            block[...] = m[top:end, top:end]
            inverse = eliminate(block)
            if end < order:
                right = dot_full(inverse, m[top:end, end:], ((1,), (0,)))
                for t in range(s + 1, steps):
                    left = right[:, t * tile - end : (t + 1) * tile - end]
                    span = slice(t * tile, (t + 1) * tile)
                    m[span, t * tile :] -= dot_full(
                        left, right[:, t * tile - end :], ((0,), (0,))
                    )
                    m[span, top:end] = -dot_full(left, inverse, ((0,), (0,)))
            m[top:end, top:end] = inverse
            if s > 0:
                done = dot_full(inverse, m[top:end, :top], ((1,), (0,)))
                m[top:end, :top] = done
                for t in range(s + 1, steps):
                    span = slice(t * tile, (t + 1) * tile)
                    left = right[:, t * tile - end : (t + 1) * tile - end]
                    m[span, :top] -= dot_full(left, done, ((0,), (0,)))
            if end < order:
                m[top:end, end:] = jnp.zeros((tile, order - end), F32)
        head, tail = split(m[...])
        high[...] = head
        low[...] = tail

    return pl.pallas_call(
        kernel,
        in_specs=[pl.BlockSpec(memory_space=pltpu.VMEM)],
        out_specs=[pl.BlockSpec(memory_space=pltpu.VMEM)] * 2,
        out_shape=[jax.ShapeDtypeStruct((order, order), BF16)] * 2,
        scratch_shapes=[pltpu.VMEM((order, order), F32), pltpu.VMEM((tile, tile), F32)],
        compiler_params=pltpu.CompilerParams(vmem_limit_bytes=VMEM_LIMIT),
        cost_estimate=cost(100e9, order * order * 8),
        name="inverse_factor",
    )(pivot)


def solve_rows(gathered, high, low, column_index):
    columns, rows, local = gathered.shape
    order = high.shape[0]
    tile = 128
    pieces = local // tile
    step = 256

    def kernel(me, f, h, l, out_h, out_l, out_f, acc):
        total = jnp.zeros((step, order), F32)
        for c in range(columns):
            fh, fl = split(f[c])
            spans = [
                slice((n * columns + c) * tile, (n * columns + c + 1) * tile) for n in range(pieces)
            ]
            gh = jnp.concatenate([h[:, s] for s in spans], axis=1)
            gl = jnp.concatenate([l[:, s] for s in spans], axis=1)
            total += dot_nt(fh, gh) + (dot_nt(fh, gl) + dot_nt(fl, gh))
        acc[...] = total
        xh, xl = split(total)
        out_h[...] = xh
        out_l[...] = xl
        for n in range(pieces):
            at = pl.multiple_of((n * columns + me[0]) * tile, tile)
            out_f[n] = acc[:, pl.ds(at, tile)]

    return pl.pallas_call(
        kernel,
        grid_spec=pltpu.PrefetchScalarGridSpec(
            num_scalar_prefetch=1,
            grid=(rows // step,),
            in_specs=[
                pl.BlockSpec((columns, step, local), lambda r, *_: (0, r, 0)),
                pl.BlockSpec((order, order), lambda r, *_: (0, 0)),
                pl.BlockSpec((order, order), lambda r, *_: (0, 0)),
            ],
            out_specs=[
                pl.BlockSpec((step, order), lambda r, *_: (r, 0)),
                pl.BlockSpec((step, order), lambda r, *_: (r, 0)),
                pl.BlockSpec((pieces, step, tile), lambda r, *_: (0, r, 0)),
            ],
            scratch_shapes=[pltpu.VMEM((step, order), F32)],
        ),
        out_shape=[
            jax.ShapeDtypeStruct((rows, order), BF16),
            jax.ShapeDtypeStruct((rows, order), BF16),
            jax.ShapeDtypeStruct((pieces, rows, tile), F32),
        ],
        compiler_params=params(),
        cost_estimate=cost(6 * rows * order * order, rows * order * 8),
        name="solve_rows",
    )(column_index, gathered, high, low)


def solve_columns(rows, high, low, places):
    blocks, cols, tile, lanes = rows.shape
    order = high.shape[0]
    wide = 4
    deep = 256

    def kernel(f, h, l, out_h, out_l):
        full = jnp.concatenate(
            [
                jnp.concatenate([f[places[b], p] for p in range(wide)], axis=1)
                for b in range(order // tile)
            ],
            axis=0,
        )
        fh, fl = split(full)
        for r in range(order // deep):
            span, depth = slice(r * deep, (r + 1) * deep), (r + 1) * deep
            lh, ll = h[span, :depth], l[span, :depth]
            x = dot(lh, fh[:depth]) + (dot(lh, fl[:depth]) + dot(ll, fh[:depth]))
            xh, xl = split(x)
            out_h[span, :] = xh
            out_l[span, :] = xl

    return pl.pallas_call(
        kernel,
        grid=(cols // wide,),
        in_specs=[
            pl.BlockSpec((blocks, wide, tile, lanes), lambda g: (0, g, 0, 0)),
            pl.BlockSpec((order, order), lambda g: (0, 0)),
            pl.BlockSpec((order, order), lambda g: (0, 0)),
        ],
        out_specs=[pl.BlockSpec((order, wide * lanes), lambda g: (0, g))] * 2,
        out_shape=[jax.ShapeDtypeStruct((order, cols * lanes), BF16)] * 2,
        compiler_params=params(),
        cost_estimate=cost(4 * order * order * cols * lanes, order * cols * lanes * 8),
        name="solve_columns",
    )(rows, high, low)


def own_part(child, half, own_maps, diag, where, left, right, panel):
    _, _, rows, tile, cols, lanes = child.shape
    rowmap, colmap = own_maps
    xh, xl = left
    ch, cl = right
    order = xh.shape[1]
    count = panel.shape[0]
    block = min(4, rows)

    def kernel(half_ref, map_ref, where_ref, u, c, d, lh, ll, rh, rl, pan, out, flat):
        g, n = pl.program_id(0), pl.program_id(1)
        columns = c[...]
        for b in range(block):
            j = n * block + b

            def body(step, carry):
                for r in range(SUB):
                    o = step * SUB + r
                    at = pl.multiple_of((b * tile + o) * SUB, SUB)
                    flat[pl.ds(at, SUB), :] = gathered_row(
                        map_ref[j, o], lambda s: u[0, 0, b, s], columns
                    )
                return carry

            lax.fori_loop(0, tile // SUB, body, 0)
            for p in range(SUB):
                @pl.when(where_ref[j] == g * SUB + p)
                def _():
                    eye = lax.broadcasted_iota(jnp.int32, (tile, lanes), 0) == (
                        lax.broadcasted_iota(jnp.int32, (tile, lanes), 1)
                    )
                    flat[pl.ds(b * tile * SUB + p, tile, SUB), :] += jnp.where(eye, d[b], 0.0)
        lhs_h, lhs_l = lh[...], ll[...]
        for pair in range(SUB // 2):
            span = slice(pair * 2 * lanes, (pair + 1) * 2 * lanes)
            update = dot(lhs_h, rh[:, span]) + (dot(lhs_h, rl[:, span]) + dot(lhs_l, rh[:, span]))
            for b in range(block):
                for side in range(2):
                    at = pl.ds(b * tile * SUB + 2 * pair + side, tile, SUB)
                    part = update[b * tile : (b + 1) * tile, side * lanes : (side + 1) * lanes]
                    flat[at, :] -= part

        @pl.when(g == 0)
        def _():
            for b in range(block):
                for p in range(count):
                    flat[pl.ds(b * tile * SUB + p, tile, SUB), :] = pan[
                        p, b * tile : (b + 1) * tile, :
                    ]

        out[...] = flat[...].reshape(out.shape)

    return pl.pallas_call(
        kernel,
        grid_spec=pltpu.PrefetchScalarGridSpec(
            num_scalar_prefetch=3,
            grid=(cols // SUB, rows // block),
            in_specs=[
                pl.BlockSpec(
                    (1, 1, block, tile, SUB, lanes), lambda g, n, h, *_: (0, h[0], n, 0, g, 0)
                ),
                pl.BlockSpec((SUB, lanes), lambda g, n, *_: (g, 0)),
                pl.BlockSpec((block, 1, lanes), lambda g, n, *_: (n, 0, 0)),
                pl.BlockSpec((block * tile, order), lambda g, n, *_: (n, 0)),
                pl.BlockSpec((block * tile, order), lambda g, n, *_: (n, 0)),
                pl.BlockSpec((order, SUB * lanes), lambda g, n, *_: (0, g)),
                pl.BlockSpec((order, SUB * lanes), lambda g, n, *_: (0, g)),
                pl.BlockSpec((count, block * tile, lanes), lambda g, n, *_: (0, n, 0)),
            ],
            out_specs=pl.BlockSpec((1, block, tile, SUB, lanes), lambda g, n, *_: (0, n, 0, g, 0)),
            scratch_shapes=[pltpu.VMEM((block * tile * SUB, lanes), F32)],
        ),
        out_shape=jax.ShapeDtypeStruct((1, rows, tile, cols, lanes), F32),
        compiler_params=params(2),
        cost_estimate=cost(
            6 * rows * tile * order * cols * lanes, rows * tile * cols * lanes * 8
        ),
        name="own_part",
    )(half, rowmap, where, child, colmap, diag[:, None, :], xh, xl, ch, cl, panel)


def add_first(front, block, rowmap, colmap):
    _, _, tile, cols, lanes = front.shape

    def kernel(map_ref, before, u, c, out):
        columns = c[...]

        def body(step, carry):
            for r in range(SUB):
                o = step * SUB + r
                value = gathered_row(map_ref[0, o], lambda s: u[0, s], columns)
                out[0, 0, o] = before[0, 0, o] + value
            return carry

        lax.fori_loop(0, tile // SUB, body, 0)

    spec = pl.BlockSpec((1, 1, tile, SUB, lanes), lambda g, *_: (0, 0, 0, g, 0))
    return pl.pallas_call(
        kernel,
        grid_spec=pltpu.PrefetchScalarGridSpec(
            num_scalar_prefetch=1,
            grid=(cols // SUB,),
            in_specs=[
                spec,
                pl.BlockSpec((1, tile, SUB, lanes), lambda g, *_: (0, 0, g, 0)),
                pl.BlockSpec((SUB, lanes), lambda g, *_: (g, 0)),
            ],
            out_specs=spec,
        ),
        out_shape=jax.ShapeDtypeStruct(front.shape, F32),
        input_output_aliases={1: 0},
        compiler_params=params(),
        cost_estimate=cost(0, tile * cols * lanes * 12),
        name="add_first",
    )(rowmap, front, block, colmap)


def add_tiles(front, sources, picks, stands, rowmap, colmap, first, count):
    _, _, tile, cols, lanes = front.shape
    width = len(sources)
    groups = cols // SUB
    picks, stands = picks.reshape(-1), stands.reshape(-1)

    def entry(slot, n, g):
        return (slot * count + n) * groups + g

    def kernel(map_ref, picks_ref, stands_ref, before, *refs):
        tiles, (c, out, flat) = refs[:width], refs[width:]
        n, g = pl.program_id(0), pl.program_id(1)
        columns = c[...]
        for slot in range(width):
            stand = stands_ref[entry(slot, n, g)]
            p = stand // 2

            @pl.when((stand >= 0) & (stand % 2 == 0))
            def _():
                flat[pl.ds(p, tile, SUB), :] = tiles[slot][0]

            @pl.when((stand >= 0) & (stand % 2 == 1))
            def _():
                flat[pl.ds(p, tile, SUB), :] = tiles[slot][0].T

        def body(step, carry):
            for r in range(SUB):
                o = step * SUB + r
                value = gathered_row(
                    map_ref[n + first, o],
                    lambda s: flat[pl.ds(pl.multiple_of(s * SUB, SUB), SUB), :],
                    columns,
                )
                out[0, 0, o] = before[0, 0, o] + value
            return carry

        lax.fori_loop(0, tile // SUB, body, 0)

    spec = pl.BlockSpec((1, 1, tile, SUB, lanes), lambda n, g, *_: (0, n + first, 0, g, 0))

    def tile_spec(slot):
        return pl.BlockSpec((1, tile, lanes), lambda n, g, m, k, t: (k[entry(slot, n, g)], 0, 0))

    return pl.pallas_call(
        kernel,
        grid_spec=pltpu.PrefetchScalarGridSpec(
            num_scalar_prefetch=3,
            grid=(count, groups),
            in_specs=[spec]
            + [tile_spec(slot) for slot in range(width)]
            + [pl.BlockSpec((SUB, lanes), lambda n, g, *_: (g, 0))],
            out_specs=spec,
            scratch_shapes=[pltpu.VMEM((tile * SUB, lanes), F32)],
        ),
        out_shape=jax.ShapeDtypeStruct(front.shape, F32),
        input_output_aliases={3: 0},
        compiler_params=params(2),
        cost_estimate=cost(0, count * tile * cols * lanes * 12),
        name="add_tiles",
    )(rowmap, picks, stands, front, *sources, colmap)


def triangle(row):
    return row * (row - 1) // 2


def lower_tables(exchanged, first, last, rows, parity, start, count):
    groups = rows // (SUB // 2)
    slot, n, g = np.meshgrid(
        np.arange(SUB // 2), np.arange(start, start + count), np.arange(groups), indexing="ij"
    )
    i = g * (SUB // 2) + slot
    row, col = (i, n) if exchanged else (n, i)
    mine = (row >= first) & (row < last) & (col >= 1)
    mine &= (col < row) if exchanged else (col <= row)
    picks = np.where(mine, triangle(row) - triangle(first) + col - 1, 0)
    flat = mine.reshape(SUB // 2, -1)
    held = picks.reshape(SUB // 2, -1).copy()
    for step in range(1, held.shape[1]):
        held[:, step] = np.where(flat[:, step], held[:, step], held[:, step - 1])
    stands = jnp.where(mine, 2 * (2 * slot + parity) + int(exchanged), -1)
    return held.reshape(mine.shape).astype(np.int32), stands.astype(jnp.int32)


def cross_tables(rows, parity, start, count):
    groups = rows // (SUB // 2)
    slot, n, g = np.meshgrid(
        np.arange(SUB // 2), np.arange(count), np.arange(groups), indexing="ij"
    )
    i = g * (SUB // 2) + slot
    picks = np.where(i >= 1, n * (rows - 1) + i - 1, n * (rows - 1))
    stands = jnp.where(i >= 1, 2 * (2 * slot + parity), -1)
    return picks.astype(np.int32), stands.astype(jnp.int32)


def on_device(child_update, child_map, parent_diag):
    grid_size = lax.axis_size(("cube", "row"))
    half_grid = grid_size // 2
    columns = lax.axis_size("col")
    position = lax.axis_index(("cube", "row"))
    column_index = lax.axis_index("col")
    sibling = position // half_grid
    within = position % half_grid
    _, _, rows, tile, cols, lanes = child_update.shape
    distance = half_grid.bit_length() - 1
    pivots = K // tile
    local = pivots // columns
    mirrored = (
        grid_size == pivots
        and half_grid == columns
        and lax.axis_size("row") == half_grid
        and cols == 2 * rows
    )
    own = sibling.astype(jnp.int32)[None]
    other = 1 - own

    starts = tile * jnp.arange(rows * grid_size, dtype=jnp.int32)
    sources = jnp.stack(
        [inverse_map(child_map[e].reshape(-1, tile), starts) for e in range(2)]
    )

    def row_maps(child):
        of = lax.dynamic_index_in_dim(sources, child, 0, keepdims=False)
        of = of.reshape(rows, 2, half_grid, tile)
        return lax.dynamic_index_in_dim(of, within, 2, keepdims=False)

    def col_maps(child):
        of = lax.dynamic_index_in_dim(sources, child, 0, keepdims=False)
        of = of.reshape(cols, columns, tile)
        return lax.dynamic_index_in_dim(of, column_index, 1, keepdims=False)

    own_halves, other_halves = row_maps(sibling), row_maps(1 - sibling)
    own_cols, other_cols = col_maps(sibling), col_maps(1 - sibling)
    own_rows = lax.dynamic_index_in_dim(own_halves, sibling, 1, keepdims=False)
    other_rows = lax.dynamic_index_in_dim(other_halves, sibling, 1, keepdims=False)
    trailing_cols = jnp.where(jnp.arange(cols)[:, None] < local, -1, other_cols)

    blocks = grid_size * jnp.arange(rows, dtype=jnp.int32) + position
    diag_tiles = parent_diag.reshape(-1, tile)

    def on_diagonal(block_rows):
        offset = block_rows - column_index
        return jnp.where(offset % columns == 0, offset // columns, -1).astype(jnp.int32)

    diag_rows = diag_tiles[blocks]

    panel_sent = pack_panel(child_update, other, local)
    panel_came = swapped(panel_sent, ("cube", "row"), distance)
    if mirrored:
        near = 1 + (rows * 11) // 16
        cuts = [(1, near), (near, rows)]
        lower_sent = [pack_lower(child_update, other, other, a, b) for a, b in cuts]
        pivot_sent = child_update[0, :, 0]
        pairs = [
            (r * columns + c, c * columns + r) for r in range(half_grid) for c in range(columns)
        ]
        lower_a = swapped(lower_sent[0], ("cube", "row"), distance)
        pivot_came = swapped(after(pivot_sent, panel_came), ("cube", "row"), distance)
        turned_a = lax.ppermute(lower_a, ("row", "col"), pairs)
        lower_b = swapped(after(lower_sent[1], lower_a), ("cube", "row"), distance)
        turned_b = lax.ppermute(after(lower_b, turned_a), ("row", "col"), pairs)
        sent = pack_cross(child_update, other, own)
        chain = [pivot_came, lower_b]
    else:
        pivot_sent = lax.dynamic_slice_in_dim(child_update[0, :, 0], 1 - sibling, 1, 0)
        pivot_came = swapped(after(pivot_sent, panel_came), ("cube", "row"), distance)
        sent = pack_all(child_update, other)
        chain = [panel_came, pivot_came]
    per = -(-(rows - 1) // 5)
    spans = [(at, min(per, rows - at)) for at in range(1, rows, per)]
    came = []
    for at, count in spans:
        part = after(sent[at - 1 : at - 1 + count], chain[-2])
        came.append(swapped(part, ("cube", "row"), distance))
        chain.append(came[-1])

    panel_own = pack_panel(child_update, own, local)

    def placed(tiles, row_map, col_map):
        offsets = jnp.arange(tile, dtype=jnp.int32)
        row_hot = (row_map[:, :, None] == offsets).astype(F32)
        col_hot = (col_map[:local, :, None] == offsets).astype(F32)
        done = jnp.einsum("jos,jpsv->jpov", row_hot, tiles, precision=lax.Precision.HIGHEST)
        return jnp.einsum("jpov,pqv->jopq", done, col_hot, precision=lax.Precision.HIGHEST)

    hits = on_diagonal(blocks)[:, None] == jnp.arange(local)
    eye = jnp.eye(tile, dtype=bool)[None, :, None, :] & hits[:, None, :, None]
    front_panel = placed(panel_own, own_rows, own_cols)
    front_panel += placed(panel_came, other_rows, other_cols)
    front_panel += jnp.where(eye, diag_rows[:, :, None, None], 0.0)

    pivot = lax.all_gather(front_panel[0], ("cube", "row", "col"), axis=0, tiled=False)
    pivot = pivot.reshape(grid_size, columns, tile, local, tile)[:pivots]
    pivot = jnp.transpose(pivot, (0, 2, 3, 1, 4)).reshape(K, K)
    high, low = inverse_factor(pivot, tile)

    gathered = lax.all_gather(
        front_panel.reshape(rows * tile, local * tile), "col", axis=0, tiled=False
    )
    left_h, left_l, panel = solve_rows(
        gathered, high, low, column_index.astype(jnp.int32)[None]
    )

    if mirrored:
        block_rows = half_grid * jnp.arange(2, dtype=jnp.int32) + within
        pivot_rows = place_rows(
            pivot_sent,
            pivot_came,
            ((own_halves[0], own_cols), (other_halves[0], other_cols)),
            diag_tiles[block_rows],
            on_diagonal(block_rows),
        )
        pivot_rows = lax.all_gather(pivot_rows, "row", axis=0, tiled=True)
        places = [2 * (b % half_grid) + b // half_grid for b in range(pivots)]
        first = lax.dynamic_slice_in_dim(pivot_came, sibling, 1, 0)
    else:
        pivot_rows = place_rows(
            lax.dynamic_slice_in_dim(child_update[0, :, 0], sibling, 1, 0),
            pivot_came,
            ((own_rows[:1], own_cols), (other_rows[:1], other_cols)),
            diag_rows[:1],
            on_diagonal(blocks[:1]),
        )
        mine = (jnp.arange(pivots) == position)[:, None, None, None]
        pivot_rows = lax.psum(jnp.where(mine, pivot_rows, 0.0), ("cube", "row"))
        places = list(range(pivots))
        first = pivot_came
    right_h, right_l = solve_columns(pivot_rows, high, low, places)

    front = own_part(
        child_update,
        own,
        (own_rows, own_cols),
        diag_rows,
        on_diagonal(blocks),
        (left_h, left_l),
        (right_h, right_l),
        panel,
    )
    front = add_first(front, first, other_rows[:1], trailing_cols)
    for (at, count), array in zip(spans, came):
        flat = array.reshape(-1, tile, tile)
        if mirrored:
            half = SUB // 2
            picks, stands = [], []
            arrays = []
            tables = [(flat, cross_tables(rows, 1 - sibling, at, count))]
            for exchanged, group in ((False, (lower_a, lower_b)), (True, (turned_a, turned_b))):
                for (a, b), source in zip(cuts, group):
                    tables.append(
                        (source, lower_tables(exchanged, a, b, rows, sibling, at, count))
                    )
            for source, (pick, stand) in tables:
                arrays += [source] * half
                picks.append(pick)
                stands.append(stand)
            picks, stands = jnp.concatenate(picks), jnp.concatenate(stands)
        else:
            arrays = [flat] * SUB
            shape = (SUB, count, cols // SUB)
            slot, n, g = (lax.broadcasted_iota(jnp.int32, shape, axis) for axis in range(3))
            picks, stands = n * cols + g * SUB + slot, 2 * slot
        front = add_tiles(front, arrays, picks, stands, other_rows, trailing_cols, at, count)
    return front


def solution(mesh):
    return jax.shard_map(
        on_device,
        mesh=mesh,
        in_specs=(P(("cube", "row"), None, None, None, "col", None), P(), P()),
        out_specs=P(("cube", "row"), None, None, "col", None),
        check_vma=False,
    )
```

```python
import jax
import jax.numpy as jnp
import numpy as np
from jax import lax
from jax.experimental import pallas as pl
from jax.experimental.pallas import tpu as pltpu
from jax.sharding import PartitionSpec as P

K = 1024
F32 = jnp.float32
BF16 = jnp.bfloat16
SUB = 8
BATCH = 32
WEIGHT = 0.01
VMEM_LIMIT = 56 * 1024 * 1024


def params(steps=1):
    return pltpu.CompilerParams(
        dimension_semantics=("arbitrary",) * steps, vmem_limit_bytes=VMEM_LIMIT
    )


def cost(flops, moved):
    return pl.CostEstimate(
        flops=int(flops * WEIGHT), bytes_accessed=int(moved * WEIGHT), transcendentals=0
    )


def swapped(value, axis, distance):
    mask = 2**distance
    pairs = [(source, source ^ mask) for source in range(lax.axis_size(axis))]
    return lax.ppermute(value, axis, pairs)


def after(value, *others):
    return lax.optimization_barrier((value,) + others)[0]


def inverse_map(values, starts):
    tile = values.shape[-1]
    offsets = jnp.arange(tile, dtype=jnp.int32)
    hit = (values - starts[:, None])[:, None, :] == offsets[None, :, None]
    return jnp.sum(jnp.where(hit, offsets[None, None, :] + 1, 0), axis=-1).astype(jnp.int32) - 1


def split(value):
    high = value.astype(BF16)
    return high, (value - high.astype(F32)).astype(BF16)


def dot(a, b):
    return jnp.dot(a, b, preferred_element_type=F32)


def dot_nt(a, b):
    return lax.dot_general(a, b, (((1,), (1,)), ((), ())), preferred_element_type=F32)


def dot_full(a, b, dims):
    return lax.dot_general(
        a, b, (dims, ((), ())), precision=lax.Precision.HIGHEST, preferred_element_type=F32
    )


def pack_panel(child, half, count):
    _, _, rows, tile, _, lanes = child.shape
    block = min(4, rows)

    def kernel(half_ref, raw, out):
        flat = raw.reshape(block * tile * SUB, lanes)
        for b in range(block):
            for p in range(count):
                out[b, p] = flat[pl.ds(b * tile * SUB + p, tile, SUB), :]

    return pl.pallas_call(
        kernel,
        grid_spec=pltpu.PrefetchScalarGridSpec(
            num_scalar_prefetch=1,
            grid=(rows // block,),
            in_specs=[
                pl.BlockSpec((1, 1, block, tile, SUB, lanes), lambda j, h: (0, h[0], j, 0, 0, 0))
            ],
            out_specs=pl.BlockSpec((block, count, tile, lanes), lambda j, h: (j, 0, 0, 0)),
        ),
        out_shape=jax.ShapeDtypeStruct((rows, count, tile, lanes), F32),
        compiler_params=params(),
        cost_estimate=cost(0, rows * tile * lanes * 4 * (SUB + count)),
        name="pack_panel",
    )(half, child)


def pack_cross(child, half, parity):
    _, _, rows, tile, cols, lanes = child.shape
    pairs = cols // 2

    def kernel(half_ref, parity_ref, raw, out):
        for i in range(1, pairs):
            at = pl.ds(2 * i + parity_ref[0], tile, cols)
            out[0, i - 1] = raw.reshape(tile * cols, lanes)[at, :]

    return pl.pallas_call(
        kernel,
        grid_spec=pltpu.PrefetchScalarGridSpec(
            num_scalar_prefetch=2,
            grid=(rows - 1,),
            in_specs=[
                pl.BlockSpec(
                    (1, 1, 1, tile, cols, lanes), lambda j, h, b: (0, h[0], j + 1, 0, 0, 0)
                )
            ],
            out_specs=pl.BlockSpec((1, pairs - 1, tile, lanes), lambda j, h, b: (j, 0, 0, 0)),
        ),
        out_shape=jax.ShapeDtypeStruct((rows - 1, pairs - 1, tile, lanes), F32),
        compiler_params=params(),
        cost_estimate=cost(0, rows * tile * lanes * 4 * (cols + pairs)),
        name="pack_cross",
    )(half, parity, child)


def pack_lower(child, half, parity, first, last):
    _, _, _, tile, cols, lanes = child.shape
    base = first * (first - 1) // 2
    count = last * (last - 1) // 2 - base

    def kernel(half_ref, parity_ref, raw, out):
        j = pl.program_id(0) + first
        start = j * (j - 1) // 2 - base - 1
        for i in range(1, last):
            @pl.when(i <= j)
            def _():
                at = pl.ds(2 * i + parity_ref[0], tile, cols)
                out[start + i] = raw.reshape(tile * cols, lanes)[at, :]

    return pl.pallas_call(
        kernel,
        grid_spec=pltpu.PrefetchScalarGridSpec(
            num_scalar_prefetch=2,
            grid=(last - first,),
            in_specs=[
                pl.BlockSpec(
                    (1, 1, 1, tile, cols, lanes), lambda j, h, b: (0, h[0], j + first, 0, 0, 0)
                )
            ],
            out_specs=pl.BlockSpec((count, tile, lanes), lambda j, h, b: (0, 0, 0)),
        ),
        out_shape=jax.ShapeDtypeStruct((count, tile, lanes), F32),
        compiler_params=params(),
        cost_estimate=cost(0, tile * lanes * 4 * ((last - first) * cols + count)),
        name="pack_lower",
    )(half, parity, child)


def pack_all(child, half):
    _, _, rows, tile, cols, lanes = child.shape

    def kernel(half_ref, raw, out):
        for p in range(cols):
            out[0, p] = raw.reshape(tile * cols, lanes)[pl.ds(p, tile, cols), :]

    return pl.pallas_call(
        kernel,
        grid_spec=pltpu.PrefetchScalarGridSpec(
            num_scalar_prefetch=1,
            grid=(rows - 1,),
            in_specs=[
                pl.BlockSpec((1, 1, 1, tile, cols, lanes), lambda j, h: (0, h[0], j + 1, 0, 0, 0))
            ],
            out_specs=pl.BlockSpec((1, cols, tile, lanes), lambda j, h: (j, 0, 0, 0)),
        ),
        out_shape=jax.ShapeDtypeStruct((rows - 1, cols, tile, lanes), F32),
        compiler_params=params(),
        cost_estimate=cost(0, rows * tile * lanes * 8 * cols),
        name="pack_all",
    )(half, child)


def place_block(rowmap, row, load, columns, store):
    tile = columns.shape[-1]
    live = columns >= 0
    lanes = jnp.maximum(columns, 0)

    def body(step, carry):
        index = [rowmap[row, step * BATCH + r] for r in range(BATCH)]
        values = [load(jnp.maximum(i, 0)) for i in index]
        values = [
            jnp.take_along_axis(v, lanes, axis=1, mode="promise_in_bounds") for v in values
        ]
        store(step * BATCH, [jnp.where(live & (i >= 0), v, 0.0) for i, v in zip(index, values)])
        return carry

    lax.fori_loop(0, tile // BATCH, body, 0)


def place_rows(first, second, maps, diag, where):
    count, tile, cols, lanes = first.shape
    (rows0, cols0), (rows1, cols1) = maps

    def kernel(rows0_ref, rows1_ref, where_ref, u0, u1, c0, c1, d, out, flat):
        n, g = pl.program_id(0), pl.program_id(1)

        def put(at, values):
            for r, value in enumerate(values):
                flat[pl.ds(pl.multiple_of((at + r) * SUB, SUB), SUB), :] = value

        def add(at, values):
            spots = [pl.ds(pl.multiple_of((at + r) * SUB, SUB), SUB) for r in range(BATCH)]
            values = [flat[spot, :] + value for spot, value in zip(spots, values)]
            for spot, value in zip(spots, values):
                flat[spot, :] = value

        place_block(rows0_ref, n, lambda s: u0[0, s], c0[...], put)
        place_block(rows1_ref, n, lambda s: u1[0, s], c1[...], add)
        for p in range(SUB):
            out[0, p] = flat[pl.ds(p, tile, SUB), :]

            @pl.when(where_ref[n] == g * SUB + p)
            def _():
                eye = lax.broadcasted_iota(jnp.int32, (tile, lanes), 0) == (
                    lax.broadcasted_iota(jnp.int32, (tile, lanes), 1)
                )
                out[0, p] += jnp.where(eye, d[0], 0.0)

    return pl.pallas_call(
        kernel,
        grid_spec=pltpu.PrefetchScalarGridSpec(
            num_scalar_prefetch=3,
            grid=(count, cols // SUB),
            in_specs=[
                pl.BlockSpec((1, tile, SUB, lanes), lambda n, g, *_: (n, 0, g, 0)),
                pl.BlockSpec((1, tile, SUB, lanes), lambda n, g, *_: (n, 0, g, 0)),
                pl.BlockSpec((SUB, lanes), lambda n, g, *_: (g, 0)),
                pl.BlockSpec((SUB, lanes), lambda n, g, *_: (g, 0)),
                pl.BlockSpec((1, 1, lanes), lambda n, g, *_: (n, 0, 0)),
            ],
            out_specs=pl.BlockSpec((1, SUB, tile, lanes), lambda n, g, *_: (n, g, 0, 0)),
            scratch_shapes=[pltpu.VMEM((tile * SUB, lanes), F32)],
        ),
        out_shape=jax.ShapeDtypeStruct((count, cols, tile, lanes), F32),
        compiler_params=params(2),
        cost_estimate=cost(0, count * cols * tile * lanes * 12),
        name="place_rows",
    )(rows0, rows1, where, first, second, cols0, cols1, diag[:, None, :])


def eliminate(block):
    tile = block.shape[0]
    lane = lax.broadcasted_iota(jnp.int32, (1, tile), 1)
    sub = lax.broadcasted_iota(jnp.int32, (tile, 1), 0)

    def at_lane(value, j):
        index = jnp.full(value.shape, j, jnp.int32)
        return jnp.take_along_axis(value, index, axis=1, mode="promise_in_bounds")

    def body(j, carry):
        whole = block[...]
        row = jnp.broadcast_to(block[pl.ds(j, 1), :], (SUB, tile))
        here = lane == j
        pivot = at_lane(row, j)
        root = lax.rsqrt(pivot)
        root = root * (1.5 - 0.5 * pivot * root * root)
        row = jnp.where(here, root, row * root)[:1]
        column = jnp.where(sub > j, at_lane(whole, j), 0.0) * root[:1]
        kept = jnp.where(here & (sub > j), 0.0, whole)
        block[...] = jnp.where(sub == j, row, kept - column * row)
        return carry

    lax.fori_loop(0, tile, body, 0)
    low = lax.broadcasted_iota(jnp.int32, (tile, tile), 0) >= (
        lax.broadcasted_iota(jnp.int32, (tile, tile), 1)
    )
    return jnp.where(low, block[...], 0.0)


def inverse_factor(pivot, tile):
    order = pivot.shape[0]
    steps = order // tile

    def kernel(a, high, low, m, block):
        m[...] = a[...]
        for s in range(steps):
            top, end = s * tile, (s + 1) * tile
            block[...] = m[top:end, top:end]
            inverse = eliminate(block)
            if end < order:
                right = dot_full(inverse, m[top:end, end:], ((1,), (0,)))
                for t in range(s + 1, steps):
                    left = right[:, t * tile - end : (t + 1) * tile - end]
                    span = slice(t * tile, (t + 1) * tile)
                    m[span, t * tile :] -= dot_full(
                        left, right[:, t * tile - end :], ((0,), (0,))
                    )
                    m[span, top:end] = -dot_full(left, inverse, ((0,), (0,)))
            m[top:end, top:end] = inverse
            if s > 0:
                done = dot_full(inverse, m[top:end, :top], ((1,), (0,)))
                m[top:end, :top] = done
                for t in range(s + 1, steps):
                    span = slice(t * tile, (t + 1) * tile)
                    left = right[:, t * tile - end : (t + 1) * tile - end]
                    m[span, :top] -= dot_full(left, done, ((0,), (0,)))
            if end < order:
                m[top:end, end:] = jnp.zeros((tile, order - end), F32)
        head, tail = split(m[...])
        high[...] = head
        low[...] = tail

    return pl.pallas_call(
        kernel,
        in_specs=[pl.BlockSpec(memory_space=pltpu.VMEM)],
        out_specs=[pl.BlockSpec(memory_space=pltpu.VMEM)] * 2,
        out_shape=[jax.ShapeDtypeStruct((order, order), BF16)] * 2,
        scratch_shapes=[pltpu.VMEM((order, order), F32), pltpu.VMEM((tile, tile), F32)],
        compiler_params=pltpu.CompilerParams(vmem_limit_bytes=VMEM_LIMIT),
        cost_estimate=cost(100e9, order * order * 8),
        name="inverse_factor",
    )(pivot)


def solve_rows(gathered, high, low, column_index):
    columns, rows, local = gathered.shape
    order = high.shape[0]
    tile = 128
    pieces = local // tile
    step = 256

    def kernel(me, f, h, l, out_h, out_l, out_f, acc):
        total = jnp.zeros((step, order), F32)
        for c in range(columns):
            fh, fl = split(f[c])
            spans = [
                slice((n * columns + c) * tile, (n * columns + c + 1) * tile) for n in range(pieces)
            ]
            gh = jnp.concatenate([h[:, s] for s in spans], axis=1)
            gl = jnp.concatenate([l[:, s] for s in spans], axis=1)
            total += dot_nt(fh, gh) + (dot_nt(fh, gl) + dot_nt(fl, gh))
        acc[...] = total
        xh, xl = split(total)
        out_h[...] = xh
        out_l[...] = xl
        for n in range(pieces):
            at = pl.multiple_of((n * columns + me[0]) * tile, tile)
            out_f[n] = acc[:, pl.ds(at, tile)]

    return pl.pallas_call(
        kernel,
        grid_spec=pltpu.PrefetchScalarGridSpec(
            num_scalar_prefetch=1,
            grid=(rows // step,),
            in_specs=[
                pl.BlockSpec((columns, step, local), lambda r, *_: (0, r, 0)),
                pl.BlockSpec((order, order), lambda r, *_: (0, 0)),
                pl.BlockSpec((order, order), lambda r, *_: (0, 0)),
            ],
            out_specs=[
                pl.BlockSpec((step, order), lambda r, *_: (r, 0)),
                pl.BlockSpec((step, order), lambda r, *_: (r, 0)),
                pl.BlockSpec((pieces, step, tile), lambda r, *_: (0, r, 0)),
            ],
            scratch_shapes=[pltpu.VMEM((step, order), F32)],
        ),
        out_shape=[
            jax.ShapeDtypeStruct((rows, order), BF16),
            jax.ShapeDtypeStruct((rows, order), BF16),
            jax.ShapeDtypeStruct((pieces, rows, tile), F32),
        ],
        compiler_params=params(),
        cost_estimate=cost(6 * rows * order * order, rows * order * 8),
        name="solve_rows",
    )(column_index, gathered, high, low)


def solve_columns(parts, homes, high, low):
    _, cols, tile, lanes = parts[0].shape
    order = high.shape[0]
    wide = 4
    deep = 256
    width = len(parts)

    def kernel(home, *refs):
        f, (h, l, out_h, out_l, fh, fl) = refs[:width], refs[width:]
        number = 0
        for part in f:
            for b in range(part.shape[0]):
                block = jnp.concatenate([part[b, p] for p in range(wide)], axis=1)
                rows = pl.ds(pl.multiple_of(home[number] * tile, tile), tile)
                fh[rows, :], fl[rows, :] = split(block)
                number += 1
        for r in range(order // deep):
            span, depth = slice(r * deep, (r + 1) * deep), (r + 1) * deep
            lh, ll = h[span, :depth], l[span, :depth]
            x = dot(lh, fh[:depth]) + (dot(lh, fl[:depth]) + dot(ll, fh[:depth]))
            out_h[span, :], out_l[span, :] = split(x)

    return pl.pallas_call(
        kernel,
        grid_spec=pltpu.PrefetchScalarGridSpec(
            num_scalar_prefetch=1,
            grid=(cols // wide,),
            in_specs=[
                pl.BlockSpec((part.shape[0], wide, tile, lanes), lambda g, *_: (0, g, 0, 0))
                for part in parts
            ]
            + [pl.BlockSpec((order, order), lambda g, *_: (0, 0))] * 2,
            out_specs=[pl.BlockSpec((order, wide * lanes), lambda g, *_: (0, g))] * 2,
            scratch_shapes=[pltpu.VMEM((order, wide * lanes), BF16)] * 2,
        ),
        out_shape=[jax.ShapeDtypeStruct((order, cols * lanes), BF16)] * 2,
        compiler_params=params(),
        cost_estimate=cost(4 * order * order * cols * lanes, order * cols * lanes * 8),
        name="solve_columns",
    )(homes, *parts, high, low)


def own_part(before, child, half, own_maps, diag, where, left, right, panel, start, end):
    _, _, rows, tile, cols, lanes = child.shape
    rowmap, colmap = own_maps
    xh, xl = left
    ch, cl = right
    order = xh.shape[1]
    count = panel.shape[0]
    block = min(4, rows)

    def kernel(half_ref, map_ref, where_ref, *refs):
        u, c, d, lh, ll, rh, rl, pan, out, flat = refs[-10:]
        g, n = pl.program_id(0) + start, pl.program_id(1)
        columns = c[...]
        for b in range(block):
            j = n * block + b

            def put(at, values):
                for r, value in enumerate(values):
                    spot = pl.multiple_of((b * tile + at + r) * SUB, SUB)
                    flat[pl.ds(spot, SUB), :] = value

            place_block(map_ref, j, lambda s: u[0, 0, b, s], columns, put)
            for p in range(SUB):
                @pl.when(where_ref[j] == g * SUB + p)
                def _():
                    eye = lax.broadcasted_iota(jnp.int32, (tile, lanes), 0) == (
                        lax.broadcasted_iota(jnp.int32, (tile, lanes), 1)
                    )
                    flat[pl.ds(b * tile * SUB + p, tile, SUB), :] += jnp.where(eye, d[b], 0.0)
        lhs_h, lhs_l = lh[...], ll[...]
        for pair in range(SUB // 2):
            span = slice(pair * 2 * lanes, (pair + 1) * 2 * lanes)
            update = dot(lhs_h, rh[:, span]) + (dot(lhs_h, rl[:, span]) + dot(lhs_l, rh[:, span]))
            for b in range(block):
                for side in range(2):
                    at = pl.ds(b * tile * SUB + 2 * pair + side, tile, SUB)
                    part = update[b * tile : (b + 1) * tile, side * lanes : (side + 1) * lanes]
                    flat[at, :] -= part

        @pl.when(g == 0)
        def _():
            for b in range(block):
                for p in range(count):
                    flat[pl.ds(b * tile * SUB + p, tile, SUB), :] = pan[
                        p, b * tile : (b + 1) * tile, :
                    ]

        out[...] = flat[...].reshape(out.shape)

    held = [] if before is None else [pl.BlockSpec(memory_space=pl.ANY)]
    return pl.pallas_call(
        kernel,
        grid_spec=pltpu.PrefetchScalarGridSpec(
            num_scalar_prefetch=3,
            grid=(end - start, rows // block),
            in_specs=held
            + [
                pl.BlockSpec(
                    (1, 1, block, tile, SUB, lanes), lambda g, n, h, *_: (0, h[0], n, 0, g + start, 0)
                ),
                pl.BlockSpec((SUB, lanes), lambda g, n, *_: (g + start, 0)),
                pl.BlockSpec((block, 1, lanes), lambda g, n, *_: (n, 0, 0)),
                pl.BlockSpec((block * tile, order), lambda g, n, *_: (n, 0)),
                pl.BlockSpec((block * tile, order), lambda g, n, *_: (n, 0)),
                pl.BlockSpec((order, SUB * lanes), lambda g, n, *_: (0, g + start)),
                pl.BlockSpec((order, SUB * lanes), lambda g, n, *_: (0, g + start)),
                pl.BlockSpec((count, block * tile, lanes), lambda g, n, *_: (0, n, 0)),
            ],
            out_specs=pl.BlockSpec((1, block, tile, SUB, lanes), lambda g, n, *_: (0, n, 0, g + start, 0)),
            scratch_shapes=[pltpu.VMEM((block * tile * SUB, lanes), F32)],
        ),
        out_shape=jax.ShapeDtypeStruct((1, rows, tile, cols, lanes), F32),
        input_output_aliases={} if before is None else {3: 0},
        compiler_params=params(2),
        cost_estimate=cost(
            6 * rows * tile * order * cols * lanes, rows * tile * cols * lanes * 8
        ),
        name="own_part",
    )(half, rowmap, where, *([] if before is None else [before]), child, colmap, diag[:, None, :], xh, xl, ch, cl, panel)


def add_first(front, block, rowmap, colmap):
    _, _, tile, cols, lanes = front.shape

    def kernel(map_ref, before, u, c, out):
        def add(at, values):
            values = [before[0, 0, at + r] + value for r, value in enumerate(values)]
            for r, value in enumerate(values):
                out[0, 0, at + r] = value

        place_block(map_ref, 0, lambda s: u[0, s], c[...], add)

    spec = pl.BlockSpec((1, 1, tile, SUB, lanes), lambda g, *_: (0, 0, 0, g, 0))
    return pl.pallas_call(
        kernel,
        grid_spec=pltpu.PrefetchScalarGridSpec(
            num_scalar_prefetch=1,
            grid=(cols // SUB,),
            in_specs=[
                spec,
                pl.BlockSpec((1, tile, SUB, lanes), lambda g, *_: (0, 0, g, 0)),
                pl.BlockSpec((SUB, lanes), lambda g, *_: (g, 0)),
            ],
            out_specs=spec,
        ),
        out_shape=jax.ShapeDtypeStruct(front.shape, F32),
        input_output_aliases={1: 0},
        compiler_params=params(),
        cost_estimate=cost(0, tile * cols * lanes * 12),
        name="add_first",
    )(rowmap, front, block, colmap)


def add_tiles(front, sources, picks, stands, rowmap, colmap, first, count):
    _, _, tile, cols, lanes = front.shape
    width = len(sources)
    groups = cols // SUB
    picks, stands = (t.astype(jnp.int32).reshape(-1) for t in (picks, stands))

    def entry(slot, n, g):
        return (slot * count + n) * groups + g

    def kernel(map_ref, picks_ref, stands_ref, before, *refs):
        tiles, (c, out, flat) = refs[:width], refs[width:]
        n, g = pl.program_id(0), pl.program_id(1)
        for slot in range(width):
            stand = stands_ref[entry(slot, n, g)]
            p = stand // 2

            @pl.when((stand >= 0) & (stand % 2 == 0))
            def _():
                flat[pl.ds(p, tile, SUB), :] = tiles[slot][0]

            @pl.when((stand >= 0) & (stand % 2 == 1))
            def _():
                flat[pl.ds(p, tile, SUB), :] = tiles[slot][0].T

        def load(source):
            return flat[pl.ds(pl.multiple_of(source * SUB, SUB), SUB), :]

        def add(at, values):
            values = [before[0, 0, at + r] + value for r, value in enumerate(values)]
            for r, value in enumerate(values):
                out[0, 0, at + r] = value

        place_block(map_ref, n + first, load, c[...], add)

    spec = pl.BlockSpec((1, 1, tile, SUB, lanes), lambda n, g, *_: (0, n + first, 0, g, 0))

    def tile_spec(slot):
        return pl.BlockSpec((1, tile, lanes), lambda n, g, m, k, t: (k[entry(slot, n, g)], 0, 0))

    return pl.pallas_call(
        kernel,
        grid_spec=pltpu.PrefetchScalarGridSpec(
            num_scalar_prefetch=3,
            grid=(count, groups),
            in_specs=[spec]
            + [tile_spec(slot) for slot in range(width)]
            + [pl.BlockSpec((SUB, lanes), lambda n, g, *_: (g, 0))],
            out_specs=spec,
            scratch_shapes=[pltpu.VMEM((tile * SUB, lanes), F32)],
        ),
        out_shape=jax.ShapeDtypeStruct(front.shape, F32),
        input_output_aliases={3: 0},
        compiler_params=params(2),
        cost_estimate=cost(0, count * tile * cols * lanes * 12),
        name="add_tiles",
    )(rowmap, picks, stands, front, *sources, colmap)


def triangle(row):
    return row * (row - 1) // 2


def held_picks(picks, given):
    flat, mask = picks.reshape(picks.shape[0], -1).copy(), given.reshape(picks.shape[0], -1)
    for step in range(1, flat.shape[1]):
        flat[:, step] = np.where(mask[:, step], flat[:, step], flat[:, step - 1])
    return flat.reshape(picks.shape).astype(np.int32)


def lower_tables(exchanged, first, last, rows, parity, alone, start, count):
    groups = rows // (SUB // 2)
    slot, n, g = np.meshgrid(
        np.arange(SUB // 2), np.arange(start, start + count), np.arange(groups), indexing="ij"
    )
    i = g * (SUB // 2) + slot
    place = 2 * (2 * slot + parity)

    def inside(row, col):
        return (row >= first) & (row < last) & (col >= 1), triangle(row) - triangle(first) + col - 1

    straight, at = inside(n, i)
    straight &= i <= n
    mirror, at_mirror = inside(i, n)
    mirror &= n < i
    if exchanged:
        picks = held_picks(np.where(mirror, at_mirror, 0), mirror)
        return jnp.where(alone, 0, picks), jnp.where(mirror & ~alone, place + 1, -1)
    mine = held_picks(np.where(straight, at, 0), straight)
    both = straight | mirror
    all_of_it = held_picks(np.where(straight, at, np.where(mirror, at_mirror, 0)), both)
    stands = jnp.where(straight, place, jnp.where(mirror & alone, place + 1, -1))
    return jnp.where(alone, all_of_it, mine), stands


def cross_tables(rows, parity, start, count):
    groups = rows // (SUB // 2)
    slot, n, g = np.meshgrid(
        np.arange(SUB // 2), np.arange(count), np.arange(groups), indexing="ij"
    )
    i = g * (SUB // 2) + slot
    picks = np.where(i >= 1, n * (rows - 1) + i - 1, n * (rows - 1))
    stands = jnp.where(i >= 1, 2 * (2 * slot + parity), -1)
    return jnp.asarray(picks, jnp.int32), stands


def on_device(child_update, child_map, parent_diag):
    grid_size = lax.axis_size(("cube", "row"))
    half_grid = grid_size // 2
    columns = lax.axis_size("col")
    position = lax.axis_index(("cube", "row"))
    column_index = lax.axis_index("col")
    sibling = position // half_grid
    within = position % half_grid
    _, _, rows, tile, cols, lanes = child_update.shape
    distance = half_grid.bit_length() - 1
    pivots = K // tile
    local = pivots // columns
    mirrored = (
        grid_size == pivots
        and half_grid == columns
        and lax.axis_size("row") == half_grid
        and cols == 2 * rows
    )
    own = sibling.astype(jnp.int32)[None]
    other = 1 - own

    starts = tile * jnp.arange(rows * grid_size, dtype=jnp.int32)
    sources = jnp.stack(
        [inverse_map(child_map[e].reshape(-1, tile), starts) for e in range(2)]
    )

    def row_maps(child):
        of = lax.dynamic_index_in_dim(sources, child, 0, keepdims=False)
        of = of.reshape(rows, 2, half_grid, tile)
        return lax.dynamic_index_in_dim(of, within, 2, keepdims=False)

    def col_maps(child):
        of = lax.dynamic_index_in_dim(sources, child, 0, keepdims=False)
        of = of.reshape(cols, columns, tile)
        return lax.dynamic_index_in_dim(of, column_index, 1, keepdims=False)

    own_halves, other_halves = row_maps(sibling), row_maps(1 - sibling)
    own_cols, other_cols = col_maps(sibling), col_maps(1 - sibling)
    own_rows = lax.dynamic_index_in_dim(own_halves, sibling, 1, keepdims=False)
    other_rows = lax.dynamic_index_in_dim(other_halves, sibling, 1, keepdims=False)
    trailing_cols = jnp.where(jnp.arange(cols)[:, None] < local, -1, other_cols)

    blocks = grid_size * jnp.arange(rows, dtype=jnp.int32) + position
    diag_tiles = parent_diag.reshape(-1, tile)

    def on_diagonal(block_rows):
        offset = block_rows - column_index
        return jnp.where(offset % columns == 0, offset // columns, -1).astype(jnp.int32)

    diag_rows = diag_tiles[blocks]

    subcubes = ("cube", "row")
    spans, at = [], 1
    while at < rows:
        count = -(-3 * (rows - at) // 10)
        spans.append((at, count))
        at += count

    panel_sent = pack_panel(child_update, other, local)
    panel_own = pack_panel(after(child_update, panel_sent), own, local)
    panel_came = swapped(panel_sent, subcubes, distance)
    if mirrored:
        near = 1 + (rows * 11) // 16
        cuts = [(1, near), (near, rows)]
        lower_sent = [pack_lower(child_update, other, other, a, b) for a, b in cuts]
        pivot_sent = child_update[0, :, 0]
        panel_came = after(panel_came, panel_own, pivot_sent, lower_sent[0])
    else:
        pivot_sent = lax.dynamic_slice_in_dim(child_update[0, :, 0], 1 - sibling, 1, 0)

    def placed(tiles, row_map, col_map):
        offsets = jnp.arange(tile, dtype=jnp.int32)
        row_hot = (row_map[:, :, None] == offsets).astype(F32)
        col_hot = (col_map[:local, :, None] == offsets).astype(F32)
        done = jnp.einsum("jos,jpsv->jpov", row_hot, tiles, precision=lax.Precision.HIGHEST)
        return jnp.einsum("jpov,pqv->jopq", done, col_hot, precision=lax.Precision.HIGHEST)

    hits = on_diagonal(blocks)[:, None] == jnp.arange(local)
    eye = jnp.eye(tile, dtype=bool)[None, :, None, :] & hits[:, None, :, None]
    front_panel = placed(panel_own, own_rows, own_cols)
    front_panel += placed(panel_came, other_rows, other_cols)
    front_panel += jnp.where(eye, diag_rows[:, :, None, None], 0.0)

    pivot = lax.all_gather(front_panel[0], ("cube", "row", "col"), axis=0, tiled=False)
    gathered = lax.all_gather(
        front_panel.reshape(rows * tile, local * tile), "col", axis=0, tiled=False
    )
    pivot = pivot.reshape(grid_size, columns, tile, local, tile)[:pivots]
    pivot = jnp.transpose(pivot, (0, 2, 3, 1, 4)).reshape(K, K)

    pivot_came = swapped(after(pivot_sent, panel_came), subcubes, distance)
    if mirrored:
        pairs = [
            (r * columns + c, c * columns + r)
            for r in range(half_grid)
            for c in range(columns)
            if r != c
        ]
        lower_a = swapped(after(lower_sent[0], front_panel), subcubes, distance)
        sent = pack_cross(after(child_update, front_panel), other, own)
        pivot_came = after(pivot_came, sent, lower_sent[1])
        lower_b = swapped(after(lower_sent[1], pivot_came), subcubes, distance)
        block_rows = half_grid * jnp.arange(2, dtype=jnp.int32) + within
        pivot_rows = place_rows(
            pivot_sent,
            pivot_came,
            ((own_halves[0], own_cols), (other_halves[0], other_cols)),
            diag_tiles[block_rows],
            on_diagonal(block_rows),
        )
        across = swapped(pivot_rows, "row", 1)
        pivot = after(pivot, pivot_rows)
    else:
        sent = pack_all(child_update, other)
    high, low = inverse_factor(pivot, tile)

    came = []

    def send(number, behind):
        at, count = spans[number]
        part = after(sent[at - 1 : at - 1 + count], behind)
        came.append(swapped(part, subcubes, distance))

    if mirrored:
        lower_a = after(lower_a, high)
        turned_a = lax.ppermute(lower_a, ("row", "col"), pairs)
        send(0, lower_a)
        gathered = after(gathered, lower_a)
    left_h, left_l, panel = solve_rows(gathered, high, low, column_index.astype(jnp.int32)[None])
    if mirrored:
        across = after(across, left_h)
        beside = swapped(jnp.concatenate([pivot_rows, across]), "row", 0)
        parts = [pivot_rows, across, beside]
        homes = [block_rows ^ bits for bits in (0, 2, 1, 3)]
        first = lax.dynamic_slice_in_dim(pivot_came, sibling, 1, 0)
    else:
        for number in range(len(spans)):
            send(number, came[-2] if number > 1 else pivot_came)
        pivot_rows = place_rows(
            lax.dynamic_slice_in_dim(child_update[0, :, 0], sibling, 1, 0),
            pivot_came,
            ((own_rows[:1], own_cols), (other_rows[:1], other_cols)),
            diag_rows[:1],
            on_diagonal(blocks[:1]),
        )
        mine = (jnp.arange(pivots) == position)[:, None, None, None]
        parts = [lax.psum(jnp.where(mine, pivot_rows, 0.0), subcubes)]
        homes = [jnp.arange(pivots, dtype=jnp.int32)]
        first = pivot_came
    right_h, right_l = solve_columns(parts, jnp.concatenate(homes), high, low)
    if mirrored:
        lower_b = after(lower_b, right_h)
        turned_b = lax.ppermute(lower_b, ("row", "col"), pairs)
        send(1, lower_b)
        right_h = after(right_h, lower_b)

    front = None
    groups = cols // SUB
    for start, end in ((0, groups // 2), (groups // 2, groups)):
        front = own_part(
            front,
            child_update,
            own,
            (own_rows, own_cols),
            diag_rows,
            on_diagonal(blocks),
            (left_h, left_l),
            (right_h, right_l),
            panel,
            start,
            end,
        )
        if mirrored:
            send(len(came), front)
    front = add_first(front, first, other_rows[:1], trailing_cols)
    if mirrored:
        turned_a = after(turned_a, front)
        for number in range(len(came), len(spans)):
            came[number - 4] = after(came[number - 4], front)
            send(number, came[number - 4])
    for (at, count), array in zip(spans, came):
        flat = array.reshape(-1, tile, tile)
        if mirrored:
            half = SUB // 2
            alone = within == column_index
            tables = [(flat, cross_tables(rows, 1 - sibling, at, count))]
            for exchanged, group in ((False, (lower_a, lower_b)), (True, (turned_a, turned_b))):
                for (a, b), source in zip(cuts, group):
                    table = lower_tables(exchanged, a, b, rows, sibling, alone, at, count)
                    tables.append((source, table))
            arrays = [source for source, _ in tables for _ in range(half)]
            picks = jnp.concatenate([pick for _, (pick, _) in tables])
            stands = jnp.concatenate([stand for _, (_, stand) in tables])
        else:
            arrays = [flat] * SUB
            shape = (SUB, count, cols // SUB)
            slot, n, g = (lax.broadcasted_iota(jnp.int32, shape, axis) for axis in range(3))
            picks, stands = n * cols + g * SUB + slot, 2 * slot
        front = add_tiles(front, arrays, picks, stands, other_rows, trailing_cols, at, count)
    return front


def solution(mesh):
    return jax.shard_map(
        on_device,
        mesh=mesh,
        in_specs=(P(("cube", "row"), None, None, None, "col", None), P(), P()),
        out_specs=P(("cube", "row"), None, None, "col", None),
        check_vma=False,
    )
```

```python
import jax
import jax.numpy as jnp
import numpy as np
from jax import lax
from jax.experimental import pallas as pl
from jax.experimental.pallas import tpu as pltpu
from jax.sharding import PartitionSpec as P

K = 1024
F32 = jnp.float32
BF16 = jnp.bfloat16
SUB = 8
BATCH = 32
WEIGHT = 0.01
VMEM_LIMIT = 56 * 1024 * 1024


def params(steps=1):
    return pltpu.CompilerParams(
        dimension_semantics=("arbitrary",) * steps, vmem_limit_bytes=VMEM_LIMIT
    )


def cost(flops, moved):
    return pl.CostEstimate(
        flops=int(flops * WEIGHT), bytes_accessed=int(moved * WEIGHT), transcendentals=0
    )


def swapped(value, axis, distance):
    mask = 2**distance
    pairs = [(source, source ^ mask) for source in range(lax.axis_size(axis))]
    return lax.ppermute(value, axis, pairs)


def after(value, *others):
    return lax.optimization_barrier((value,) + others)[0]


def inverse_map(values, starts):
    tile = values.shape[-1]
    offsets = jnp.arange(tile, dtype=jnp.int32)
    hit = (values - starts[:, None])[:, None, :] == offsets[None, :, None]
    return jnp.sum(jnp.where(hit, offsets[None, None, :] + 1, 0), axis=-1).astype(jnp.int32) - 1


def split(value):
    high = value.astype(BF16)
    return high, (value - high.astype(F32)).astype(BF16)


def dot(a, b):
    return jnp.dot(a, b, preferred_element_type=F32)


def dot_nt(a, b):
    return lax.dot_general(a, b, (((1,), (1,)), ((), ())), preferred_element_type=F32)


def dot_full(a, b, dims):
    return lax.dot_general(
        a, b, (dims, ((), ())), precision=lax.Precision.HIGHEST, preferred_element_type=F32
    )


def pack_panel(child, half, count):
    _, _, rows, tile, _, lanes = child.shape
    block = min(4, rows)

    def kernel(half_ref, raw, out):
        flat = raw.reshape(block * tile * SUB, lanes)
        for b in range(block):
            for p in range(count):
                out[b, p] = flat[pl.ds(b * tile * SUB + p, tile, SUB), :]

    return pl.pallas_call(
        kernel,
        grid_spec=pltpu.PrefetchScalarGridSpec(
            num_scalar_prefetch=1,
            grid=(rows // block,),
            in_specs=[
                pl.BlockSpec((1, 1, block, tile, SUB, lanes), lambda j, h: (0, h[0], j, 0, 0, 0))
            ],
            out_specs=pl.BlockSpec((block, count, tile, lanes), lambda j, h: (j, 0, 0, 0)),
        ),
        out_shape=jax.ShapeDtypeStruct((rows, count, tile, lanes), F32),
        compiler_params=params(),
        cost_estimate=cost(0, rows * tile * lanes * 4 * (SUB + count)),
        name="pack_panel",
    )(half, child)


def pack_cross(child, half, parity):
    _, _, rows, tile, cols, lanes = child.shape
    pairs = cols // 2

    def kernel(half_ref, parity_ref, raw, out):
        for i in range(1, pairs):
            at = pl.ds(2 * i + parity_ref[0], tile, cols)
            out[0, i - 1] = raw.reshape(tile * cols, lanes)[at, :]

    return pl.pallas_call(
        kernel,
        grid_spec=pltpu.PrefetchScalarGridSpec(
            num_scalar_prefetch=2,
            grid=(rows - 1,),
            in_specs=[
                pl.BlockSpec(
                    (1, 1, 1, tile, cols, lanes), lambda j, h, b: (0, h[0], j + 1, 0, 0, 0)
                )
            ],
            out_specs=pl.BlockSpec((1, pairs - 1, tile, lanes), lambda j, h, b: (j, 0, 0, 0)),
        ),
        out_shape=jax.ShapeDtypeStruct((rows - 1, pairs - 1, tile, lanes), F32),
        compiler_params=params(),
        cost_estimate=cost(0, rows * tile * lanes * 4 * (cols + pairs)),
        name="pack_cross",
    )(half, parity, child)


def lower_start(row, first, last):
    width = last - first
    short, long = row - first, row - last
    return short * (short + 1) // 2 if long <= 0 else width * (width + 1) // 2 + long * width


def pack_lower(child, half, parity, first, last):
    _, _, rows, tile, cols, lanes = child.shape
    count = lower_start(rows, first, last)
    width = last - first

    def kernel(half_ref, parity_ref, raw, out):
        j = pl.program_id(0) + first
        short, long = j - first, j - last
        start = jnp.where(
            long <= 0, short * (short + 1) // 2, width * (width + 1) // 2 + long * width
        )
        flat = raw.reshape(tile * cols, lanes)
        for i in range(first, last):
            @pl.when(i <= j)
            def _():
                out[start + i - first] = flat[pl.ds(2 * i + parity_ref[0], tile, cols), :]

    return pl.pallas_call(
        kernel,
        grid_spec=pltpu.PrefetchScalarGridSpec(
            num_scalar_prefetch=2,
            grid=(rows - first,),
            in_specs=[
                pl.BlockSpec(
                    (1, 1, 1, tile, cols, lanes), lambda j, h, b: (0, h[0], j + first, 0, 0, 0)
                )
            ],
            out_specs=pl.BlockSpec((count, tile, lanes), lambda j, h, b: (0, 0, 0)),
        ),
        out_shape=jax.ShapeDtypeStruct((count, tile, lanes), F32),
        compiler_params=params(),
        cost_estimate=cost(0, tile * lanes * 4 * ((rows - first) * cols + count)),
        name="pack_lower",
    )(half, parity, child)


def pack_all(child, half):
    _, _, rows, tile, cols, lanes = child.shape

    def kernel(half_ref, raw, out):
        for p in range(cols):
            out[0, p] = raw.reshape(tile * cols, lanes)[pl.ds(p, tile, cols), :]

    return pl.pallas_call(
        kernel,
        grid_spec=pltpu.PrefetchScalarGridSpec(
            num_scalar_prefetch=1,
            grid=(rows - 1,),
            in_specs=[
                pl.BlockSpec((1, 1, 1, tile, cols, lanes), lambda j, h: (0, h[0], j + 1, 0, 0, 0))
            ],
            out_specs=pl.BlockSpec((1, cols, tile, lanes), lambda j, h: (j, 0, 0, 0)),
        ),
        out_shape=jax.ShapeDtypeStruct((rows - 1, cols, tile, lanes), F32),
        compiler_params=params(),
        cost_estimate=cost(0, rows * tile * lanes * 8 * cols),
        name="pack_all",
    )(half, child)


def place_block(rowmap, row, load, columns, store):
    tile = columns.shape[-1]
    live = columns >= 0
    lanes = jnp.maximum(columns, 0)

    def body(step, carry):
        index = [rowmap[row, step * BATCH + r] for r in range(BATCH)]
        values = [load(jnp.maximum(i, 0)) for i in index]
        values = [
            jnp.take_along_axis(v, lanes, axis=1, mode="promise_in_bounds") for v in values
        ]
        store(step * BATCH, [jnp.where(live & (i >= 0), v, 0.0) for i, v in zip(index, values)])
        return carry

    lax.fori_loop(0, tile // BATCH, body, 0)


def place_rows(first, second, maps, diag, where):
    count, tile, cols, lanes = first.shape
    (rows0, cols0), (rows1, cols1) = maps

    def kernel(rows0_ref, rows1_ref, where_ref, u0, u1, c0, c1, d, out, flat):
        n, g = pl.program_id(0), pl.program_id(1)

        def put(at, values):
            for r, value in enumerate(values):
                flat[pl.ds(pl.multiple_of((at + r) * SUB, SUB), SUB), :] = value

        def add(at, values):
            spots = [pl.ds(pl.multiple_of((at + r) * SUB, SUB), SUB) for r in range(BATCH)]
            values = [flat[spot, :] + value for spot, value in zip(spots, values)]
            for spot, value in zip(spots, values):
                flat[spot, :] = value

        place_block(rows0_ref, n, lambda s: u0[0, s], c0[...], put)
        place_block(rows1_ref, n, lambda s: u1[0, s], c1[...], add)
        for p in range(SUB):
            out[0, p] = flat[pl.ds(p, tile, SUB), :]

            @pl.when(where_ref[n] == g * SUB + p)
            def _():
                eye = lax.broadcasted_iota(jnp.int32, (tile, lanes), 0) == (
                    lax.broadcasted_iota(jnp.int32, (tile, lanes), 1)
                )
                out[0, p] += jnp.where(eye, d[0], 0.0)

    return pl.pallas_call(
        kernel,
        grid_spec=pltpu.PrefetchScalarGridSpec(
            num_scalar_prefetch=3,
            grid=(count, cols // SUB),
            in_specs=[
                pl.BlockSpec((1, tile, SUB, lanes), lambda n, g, *_: (n, 0, g, 0)),
                pl.BlockSpec((1, tile, SUB, lanes), lambda n, g, *_: (n, 0, g, 0)),
                pl.BlockSpec((SUB, lanes), lambda n, g, *_: (g, 0)),
                pl.BlockSpec((SUB, lanes), lambda n, g, *_: (g, 0)),
                pl.BlockSpec((1, 1, lanes), lambda n, g, *_: (n, 0, 0)),
            ],
            out_specs=pl.BlockSpec((1, SUB, tile, lanes), lambda n, g, *_: (n, g, 0, 0)),
            scratch_shapes=[pltpu.VMEM((tile * SUB, lanes), F32)],
        ),
        out_shape=jax.ShapeDtypeStruct((count, cols, tile, lanes), F32),
        compiler_params=params(2),
        cost_estimate=cost(0, count * cols * tile * lanes * 12),
        name="place_rows",
    )(rows0, rows1, where, first, second, cols0, cols1, diag[:, None, :])


def eliminate(block):
    tile = block.shape[0]
    lane = lax.broadcasted_iota(jnp.int32, (1, tile), 1)
    sub = lax.broadcasted_iota(jnp.int32, (tile, 1), 0)

    def at_lane(value, j):
        index = jnp.full(value.shape, j, jnp.int32)
        return jnp.take_along_axis(value, index, axis=1, mode="promise_in_bounds")

    def body(g, carry):
        at = pl.multiple_of(g * SUB, SUB)
        rows = block[pl.ds(at, SUB), :]
        whole = block[...].reshape(tile // SUB, SUB, tile)
        within = lax.broadcasted_iota(jnp.int32, (SUB, tile), 0)
        below = sub.reshape(tile // SUB, SUB, 1) >= at + SUB
        for r in range(SUB):
            j = at + r
            here = lane == j
            row = jnp.broadcast_to(rows[r : r + 1, :], (SUB, tile))
            pivot = at_lane(row, j)
            root = lax.rsqrt(pivot)
            root = root * (1.5 - 0.5 * pivot * root * root)
            row = jnp.where(here, root, row * root)
            column = at_lane(rows, j) * root
            under = within > r
            rows = jnp.where(
                under,
                jnp.where(here, 0.0, rows) - column * row,
                jnp.where(within == r, row, rows),
            )
            column = at_lane(whole.reshape(tile, tile), j).reshape(whole.shape) * root[None]
            whole = jnp.where(here[None], 0.0, whole) - column * row[None]
        block[...] = jnp.where(below, whole, block[...].reshape(whole.shape)).reshape(tile, tile)
        block[pl.ds(at, SUB), :] = rows
        return carry

    lax.fori_loop(0, tile // SUB, body, 0)
    low = lax.broadcasted_iota(jnp.int32, (tile, tile), 0) >= (
        lax.broadcasted_iota(jnp.int32, (tile, tile), 1)
    )
    return jnp.where(low, block[...], 0.0)


def inverse_factor(pivot, tile):
    order = pivot.shape[0]
    steps = order // tile

    def kernel(a, high, low, m, block):
        m[...] = a[...]
        for s in range(steps):
            top, end = s * tile, (s + 1) * tile
            block[...] = m[top:end, top:end]
            inverse = eliminate(block)
            if end < order:
                right = dot_full(inverse, m[top:end, end:], ((1,), (0,)))
                for t in range(s + 1, steps):
                    left = right[:, t * tile - end : (t + 1) * tile - end]
                    span = slice(t * tile, (t + 1) * tile)
                    m[span, t * tile :] -= dot_full(
                        left, right[:, t * tile - end :], ((0,), (0,))
                    )
                    m[span, top:end] = -dot_full(left, inverse, ((0,), (0,)))
            m[top:end, top:end] = inverse
            if s > 0:
                done = dot_full(inverse, m[top:end, :top], ((1,), (0,)))
                m[top:end, :top] = done
                for t in range(s + 1, steps):
                    span = slice(t * tile, (t + 1) * tile)
                    left = right[:, t * tile - end : (t + 1) * tile - end]
                    m[span, :top] -= dot_full(left, done, ((0,), (0,)))
            if end < order:
                m[top:end, end:] = jnp.zeros((tile, order - end), F32)
        head, tail = split(m[...])
        high[...] = head
        low[...] = tail

    return pl.pallas_call(
        kernel,
        in_specs=[pl.BlockSpec(memory_space=pltpu.VMEM)],
        out_specs=[pl.BlockSpec(memory_space=pltpu.VMEM)] * 2,
        out_shape=[jax.ShapeDtypeStruct((order, order), BF16)] * 2,
        scratch_shapes=[pltpu.VMEM((order, order), F32), pltpu.VMEM((tile, tile), F32)],
        compiler_params=pltpu.CompilerParams(vmem_limit_bytes=VMEM_LIMIT),
        cost_estimate=cost(100e9, order * order * 8),
        name="inverse_factor",
    )(pivot)


def solve_rows(gathered, high, low, column_index):
    columns, rows, local = gathered.shape
    order = high.shape[0]
    tile = 128
    pieces = local // tile
    step = 256

    def kernel(me, f, h, l, out_h, out_l, out_f, acc):
        total = jnp.zeros((step, order), F32)
        for c in range(columns):
            fh, fl = split(f[c])
            spans = [
                slice((n * columns + c) * tile, (n * columns + c + 1) * tile) for n in range(pieces)
            ]
            gh = jnp.concatenate([h[:, s] for s in spans], axis=1)
            gl = jnp.concatenate([l[:, s] for s in spans], axis=1)
            total += dot_nt(fh, gh) + (dot_nt(fh, gl) + dot_nt(fl, gh))
        acc[...] = total
        xh, xl = split(total)
        out_h[...] = xh
        out_l[...] = xl
        for n in range(pieces):
            at = pl.multiple_of((n * columns + me[0]) * tile, tile)
            out_f[n] = acc[:, pl.ds(at, tile)]

    return pl.pallas_call(
        kernel,
        grid_spec=pltpu.PrefetchScalarGridSpec(
            num_scalar_prefetch=1,
            grid=(rows // step,),
            in_specs=[
                pl.BlockSpec((columns, step, local), lambda r, *_: (0, r, 0)),
                pl.BlockSpec((order, order), lambda r, *_: (0, 0)),
                pl.BlockSpec((order, order), lambda r, *_: (0, 0)),
            ],
            out_specs=[
                pl.BlockSpec((step, order), lambda r, *_: (r, 0)),
                pl.BlockSpec((step, order), lambda r, *_: (r, 0)),
                pl.BlockSpec((pieces, step, tile), lambda r, *_: (0, r, 0)),
            ],
            scratch_shapes=[pltpu.VMEM((step, order), F32)],
        ),
        out_shape=[
            jax.ShapeDtypeStruct((rows, order), BF16),
            jax.ShapeDtypeStruct((rows, order), BF16),
            jax.ShapeDtypeStruct((pieces, rows, tile), F32),
        ],
        compiler_params=params(),
        cost_estimate=cost(6 * rows * order * order, rows * order * 8),
        name="solve_rows",
    )(column_index, gathered, high, low)


def solve_columns(parts, homes, high, low):
    _, cols, tile, lanes = parts[0].shape
    order = high.shape[0]
    wide = 4
    deep = 256
    width = len(parts)

    def kernel(home, *refs):
        f, (h, l, out_h, out_l, fh, fl) = refs[:width], refs[width:]
        number = 0
        for part in f:
            for b in range(part.shape[0]):
                block = jnp.concatenate([part[b, p] for p in range(wide)], axis=1)
                rows = pl.ds(pl.multiple_of(home[number] * tile, tile), tile)
                fh[rows, :], fl[rows, :] = split(block)
                number += 1
        for r in range(order // deep):
            span, depth = slice(r * deep, (r + 1) * deep), (r + 1) * deep
            lh, ll = h[span, :depth], l[span, :depth]
            x = dot(lh, fh[:depth]) + (dot(lh, fl[:depth]) + dot(ll, fh[:depth]))
            out_h[span, :], out_l[span, :] = split(x)

    return pl.pallas_call(
        kernel,
        grid_spec=pltpu.PrefetchScalarGridSpec(
            num_scalar_prefetch=1,
            grid=(cols // wide,),
            in_specs=[
                pl.BlockSpec((part.shape[0], wide, tile, lanes), lambda g, *_: (0, g, 0, 0))
                for part in parts
            ]
            + [pl.BlockSpec((order, order), lambda g, *_: (0, 0))] * 2,
            out_specs=[pl.BlockSpec((order, wide * lanes), lambda g, *_: (0, g))] * 2,
            scratch_shapes=[pltpu.VMEM((order, wide * lanes), BF16)] * 2,
        ),
        out_shape=[jax.ShapeDtypeStruct((order, cols * lanes), BF16)] * 2,
        compiler_params=params(),
        cost_estimate=cost(4 * order * order * cols * lanes, order * cols * lanes * 8),
        name="solve_columns",
    )(homes, *parts, high, low)


def own_part(before, child, half, own_maps, diag, where, left, right, panel, start, end):
    _, _, rows, tile, cols, lanes = child.shape
    rowmap, colmap = own_maps
    xh, xl = left
    ch, cl = right
    order = xh.shape[1]
    count = panel.shape[0]
    block = min(4, rows)

    def kernel(half_ref, map_ref, where_ref, *refs):
        u, c, d, lh, ll, rh, rl, pan, out, flat = refs[-10:]
        g, n = pl.program_id(0) + start, pl.program_id(1)
        columns = c[...]
        for b in range(block):
            j = n * block + b

            def put(at, values):
                for r, value in enumerate(values):
                    spot = pl.multiple_of((b * tile + at + r) * SUB, SUB)
                    flat[pl.ds(spot, SUB), :] = value

            place_block(map_ref, j, lambda s: u[0, 0, b, s], columns, put)
            for p in range(SUB):
                @pl.when(where_ref[j] == g * SUB + p)
                def _():
                    eye = lax.broadcasted_iota(jnp.int32, (tile, lanes), 0) == (
                        lax.broadcasted_iota(jnp.int32, (tile, lanes), 1)
                    )
                    flat[pl.ds(b * tile * SUB + p, tile, SUB), :] += jnp.where(eye, d[b], 0.0)
        lhs_h, lhs_l = lh[...], ll[...]
        for pair in range(SUB // 2):
            span = slice(pair * 2 * lanes, (pair + 1) * 2 * lanes)
            update = dot(lhs_h, rh[:, span]) + (dot(lhs_h, rl[:, span]) + dot(lhs_l, rh[:, span]))
            for b in range(block):
                for side in range(2):
                    at = pl.ds(b * tile * SUB + 2 * pair + side, tile, SUB)
                    part = update[b * tile : (b + 1) * tile, side * lanes : (side + 1) * lanes]
                    flat[at, :] -= part

        @pl.when(g == 0)
        def _():
            for b in range(block):
                for p in range(count):
                    flat[pl.ds(b * tile * SUB + p, tile, SUB), :] = pan[
                        p, b * tile : (b + 1) * tile, :
                    ]

        out[...] = flat[...].reshape(out.shape)

    held = [] if before is None else [pl.BlockSpec(memory_space=pl.ANY)]
    return pl.pallas_call(
        kernel,
        grid_spec=pltpu.PrefetchScalarGridSpec(
            num_scalar_prefetch=3,
            grid=(end - start, rows // block),
            in_specs=held
            + [
                pl.BlockSpec(
                    (1, 1, block, tile, SUB, lanes), lambda g, n, h, *_: (0, h[0], n, 0, g + start, 0)
                ),
                pl.BlockSpec((SUB, lanes), lambda g, n, *_: (g + start, 0)),
                pl.BlockSpec((block, 1, lanes), lambda g, n, *_: (n, 0, 0)),
                pl.BlockSpec((block * tile, order), lambda g, n, *_: (n, 0)),
                pl.BlockSpec((block * tile, order), lambda g, n, *_: (n, 0)),
                pl.BlockSpec((order, SUB * lanes), lambda g, n, *_: (0, g + start)),
                pl.BlockSpec((order, SUB * lanes), lambda g, n, *_: (0, g + start)),
                pl.BlockSpec((count, block * tile, lanes), lambda g, n, *_: (0, n, 0)),
            ],
            out_specs=pl.BlockSpec((1, block, tile, SUB, lanes), lambda g, n, *_: (0, n, 0, g + start, 0)),
            scratch_shapes=[pltpu.VMEM((block * tile * SUB, lanes), F32)],
        ),
        out_shape=jax.ShapeDtypeStruct((1, rows, tile, cols, lanes), F32),
        input_output_aliases={} if before is None else {3: 0},
        compiler_params=params(2),
        cost_estimate=cost(
            6 * rows * tile * order * cols * lanes, rows * tile * cols * lanes * 8
        ),
        name="own_part",
    )(half, rowmap, where, *([] if before is None else [before]), child, colmap, diag[:, None, :], xh, xl, ch, cl, panel)


def add_first(front, block, rowmap, colmap):
    _, _, tile, cols, lanes = front.shape

    def kernel(map_ref, before, u, c, out):
        def add(at, values):
            values = [before[0, 0, at + r] + value for r, value in enumerate(values)]
            for r, value in enumerate(values):
                out[0, 0, at + r] = value

        place_block(map_ref, 0, lambda s: u[0, s], c[...], add)

    spec = pl.BlockSpec((1, 1, tile, SUB, lanes), lambda g, *_: (0, 0, 0, g, 0))
    return pl.pallas_call(
        kernel,
        grid_spec=pltpu.PrefetchScalarGridSpec(
            num_scalar_prefetch=1,
            grid=(cols // SUB,),
            in_specs=[
                spec,
                pl.BlockSpec((1, tile, SUB, lanes), lambda g, *_: (0, 0, g, 0)),
                pl.BlockSpec((SUB, lanes), lambda g, *_: (g, 0)),
            ],
            out_specs=spec,
        ),
        out_shape=jax.ShapeDtypeStruct(front.shape, F32),
        input_output_aliases={1: 0},
        compiler_params=params(),
        cost_estimate=cost(0, tile * cols * lanes * 12),
        name="add_first",
    )(rowmap, front, block, colmap)


def add_tiles(front, entries, steps, rowmap, colmap):
    _, _, tile, cols, lanes = front.shape
    sources, picks, stands = [], [], []
    for array, pick, stand, ever in entries:
        for slot in range(len(ever)):
            if ever[slot]:
                sources.append(array)
                picks.append(pick[slot])
                stands.append(stand[slot])
    width, count = len(sources), len(steps)
    picks, stands = (jnp.concatenate(t).astype(jnp.int32) for t in (picks, stands))
    order = jnp.array([row for row, _ in steps] + [group for _, group in steps], jnp.int32)

    def kernel(map_ref, order_ref, picks_ref, stands_ref, before, *refs):
        tiles, (c, out, flat) = refs[:width], refs[width:]
        n = pl.program_id(0)
        sub = lax.broadcasted_iota(jnp.int32, (SUB, lanes), 0)
        given = jnp.zeros((SUB, lanes), jnp.int32)
        for slot in range(width):
            stand = stands_ref[slot * count + n]
            p = stand // 2
            given = jnp.where((stand >= 0) & (sub == p), 1, given)

            @pl.when((stand >= 0) & (stand % 2 == 0))
            def _():
                flat[pl.ds(p, tile, SUB), :] = tiles[slot][0]

            @pl.when((stand >= 0) & (stand % 2 == 1))
            def _():
                flat[pl.ds(p, tile, SUB), :] = tiles[slot][0].T

        def load(source):
            return flat[pl.ds(pl.multiple_of(source * SUB, SUB), SUB), :]

        def add(at, values):
            values = [before[0, 0, at + r] + value for r, value in enumerate(values)]
            for r, value in enumerate(values):
                out[0, 0, at + r] = value

        place_block(map_ref, order_ref[n], load, jnp.where(given == 1, c[...], -1), add)

    spec = pl.BlockSpec(
        (1, 1, tile, SUB, lanes), lambda n, m, o, *_: (0, o[n], 0, o[count + n], 0)
    )

    def tile_spec(slot):
        return pl.BlockSpec((1, tile, lanes), lambda n, m, o, k, t: (k[slot * count + n], 0, 0))

    return pl.pallas_call(
        kernel,
        grid_spec=pltpu.PrefetchScalarGridSpec(
            num_scalar_prefetch=4,
            grid=(count,),
            in_specs=[spec]
            + [tile_spec(slot) for slot in range(width)]
            + [pl.BlockSpec((SUB, lanes), lambda n, m, o, *_: (o[count + n], 0))],
            out_specs=spec,
            scratch_shapes=[pltpu.VMEM((tile * SUB, lanes), F32)],
        ),
        out_shape=jax.ShapeDtypeStruct(front.shape, F32),
        input_output_aliases={4: 0},
        compiler_params=params(),
        cost_estimate=cost(0, count * tile * SUB * lanes * 12),
        name="add_tiles",
    )(rowmap, order, picks, stands, front, *sources, colmap)


def held_picks(picks, given):
    held = np.where(given, picks, 0)
    for step in range(1, held.shape[1]):
        held[:, step] = np.where(given[:, step], held[:, step], held[:, step - 1])
    return held.astype(np.int32)


def straight_entry(array, first, last, rows, parity, steps):
    j, g = np.array(steps).T
    i = g[None, :] * (SUB // 2) + np.arange(SUB // 2)[:, None]
    begins = np.array([lower_start(max(row, first), first, last) for row in range(rows)])
    given = (i >= first) & (i < last) & (i <= j)
    picks = held_picks(begins[j] + i - first, given)
    place = 2 * (2 * np.arange(SUB // 2)[:, None] + parity)
    return array, jnp.asarray(picks), jnp.where(given, place, -1), given.any(axis=1)


def turned_entry(array, first, last, rows, parity, steps, used):
    j, g = np.array(steps).T
    i = g[None, :] * (SUB // 2) + np.arange(SUB // 2)[:, None]
    begins = np.array([lower_start(max(row, first), first, last) for row in range(rows)])
    given = (j >= first) & (j < last) & (i > j)
    picks = held_picks(begins[i] + j - first, given)
    place = 2 * (2 * np.arange(SUB // 2)[:, None] + parity) + 1
    stands = jnp.where(given & used, place, -1)
    return array, jnp.where(used, picks, 0), stands, given.any(axis=1)


def cross_entry(array, rows, parity, steps):
    j, g = np.array(steps).T
    i = g[None, :] * (SUB // 2) + np.arange(SUB // 2)[:, None]
    given = i >= 1
    picks = held_picks((j - j[0]) * (rows - 1) + i - 1, given)
    place = 2 * (2 * np.arange(SUB // 2)[:, None] + parity)
    return array, jnp.asarray(picks), jnp.where(given, place, -1), given.any(axis=1)


def on_device(child_update, child_map, parent_diag):
    grid_size = lax.axis_size(("cube", "row"))
    half_grid = grid_size // 2
    columns = lax.axis_size("col")
    position = lax.axis_index(("cube", "row"))
    column_index = lax.axis_index("col")
    sibling = position // half_grid
    within = position % half_grid
    _, _, rows, tile, cols, lanes = child_update.shape
    distance = half_grid.bit_length() - 1
    pivots = K // tile
    local = pivots // columns
    mirrored = (
        grid_size == pivots
        and half_grid == columns
        and lax.axis_size("row") == half_grid
        and cols == 2 * rows
    )
    own = sibling.astype(jnp.int32)[None]
    other = 1 - own

    starts = tile * jnp.arange(rows * grid_size, dtype=jnp.int32)
    sources = jnp.stack(
        [inverse_map(child_map[e].reshape(-1, tile), starts) for e in range(2)]
    )

    def row_maps(child):
        of = lax.dynamic_index_in_dim(sources, child, 0, keepdims=False)
        of = of.reshape(rows, 2, half_grid, tile)
        return lax.dynamic_index_in_dim(of, within, 2, keepdims=False)

    def col_maps(child):
        of = lax.dynamic_index_in_dim(sources, child, 0, keepdims=False)
        of = of.reshape(cols, columns, tile)
        return lax.dynamic_index_in_dim(of, column_index, 1, keepdims=False)

    own_halves, other_halves = row_maps(sibling), row_maps(1 - sibling)
    own_cols, other_cols = col_maps(sibling), col_maps(1 - sibling)
    own_rows = lax.dynamic_index_in_dim(own_halves, sibling, 1, keepdims=False)
    other_rows = lax.dynamic_index_in_dim(other_halves, sibling, 1, keepdims=False)
    trailing_cols = jnp.where(jnp.arange(cols)[:, None] < local, -1, other_cols)

    blocks = grid_size * jnp.arange(rows, dtype=jnp.int32) + position
    diag_tiles = parent_diag.reshape(-1, tile)

    def on_diagonal(block_rows):
        offset = block_rows - column_index
        return jnp.where(offset % columns == 0, offset // columns, -1).astype(jnp.int32)

    diag_rows = diag_tiles[blocks]

    subcubes = ("cube", "row")
    spans, at = [], 1
    while at < rows:
        count = -(-3 * (rows - at) // 10)
        spans.append((at, count))
        at += count

    panel_sent = pack_panel(child_update, other, local)
    panel_own = pack_panel(after(child_update, panel_sent), own, local)
    panel_came = swapped(panel_sent, subcubes, distance)
    if mirrored:
        near = spans[0][0] + spans[0][1]
        edges = [1, 2, 4, near, near + 2, rows]
        cuts = list(zip(edges[:-1], edges[1:]))
        lower_sent = [pack_lower(child_update, other, other, a, b) for a, b in cuts]
        pivot_sent = after(child_update, panel_sent)[0, :, 0]
        panel_came = after(panel_came, panel_own, pivot_sent, *lower_sent[:3])
    else:
        pivot_sent = lax.dynamic_slice_in_dim(child_update[0, :, 0], 1 - sibling, 1, 0)

    def placed(tiles, row_map, col_map):
        offsets = jnp.arange(tile, dtype=jnp.int32)
        row_hot = (row_map[:, :, None] == offsets).astype(F32)
        col_hot = (col_map[:local, :, None] == offsets).astype(F32)
        done = jnp.einsum("jos,jpsv->jpov", row_hot, tiles, precision=lax.Precision.HIGHEST)
        return jnp.einsum("jpov,pqv->jopq", done, col_hot, precision=lax.Precision.HIGHEST)

    hits = on_diagonal(blocks)[:, None] == jnp.arange(local)
    eye = jnp.eye(tile, dtype=bool)[None, :, None, :] & hits[:, None, :, None]
    front_panel = placed(panel_own, own_rows, own_cols)
    front_panel += placed(panel_came, other_rows, other_cols)
    front_panel += jnp.where(eye, diag_rows[:, :, None, None], 0.0)

    pivot = lax.all_gather(front_panel[0], ("cube", "row", "col"), axis=0, tiled=False)
    gathered = lax.all_gather(
        front_panel.reshape(rows * tile, local * tile), "col", axis=0, tiled=False
    )
    pivot = pivot.reshape(grid_size, columns, tile, local, tile)[:pivots]
    pivot = jnp.transpose(pivot, (0, 2, 3, 1, 4)).reshape(K, K)

    pivot_came = swapped(pivot_sent, subcubes, distance)
    if mirrored:
        pairs = [
            (r * columns + c, c * columns + r)
            for r in range(half_grid)
            for c in range(columns)
            if r != c
        ]
        lower = [swapped(after(part, front_panel), subcubes, distance) for part in lower_sent[:3]]
        sent = pack_cross(after(child_update, front_panel), other, own)
        pivot_came = after(pivot_came, sent, *lower_sent[3:])
        lower += [swapped(after(part, pivot_came), subcubes, distance) for part in lower_sent[3:]]
        block_rows = half_grid * jnp.arange(2, dtype=jnp.int32) + within
        pivot_rows = place_rows(
            pivot_sent,
            pivot_came,
            ((own_halves[0], own_cols), (other_halves[0], other_cols)),
            diag_tiles[block_rows],
            on_diagonal(block_rows),
        )
        across = swapped(pivot_rows, "row", 1)
        pivot = after(pivot, pivot_rows)
    else:
        sent = pack_all(child_update, other)
    high, low = inverse_factor(pivot, tile)

    came = []

    def send(number, behind):
        at, count = spans[number]
        part = after(sent[at - 1 : at - 1 + count], behind)
        came.append(swapped(part, subcubes, distance))

    if mirrored:
        lower[:2] = [after(part, high) for part in lower[:2]]
        turned = [lax.ppermute(part, ("row", "col"), pairs) for part in lower[:2]]
        send(0, lower[1])
        gathered = after(gathered, *lower[:2])
    left_h, left_l, panel = solve_rows(gathered, high, low, column_index.astype(jnp.int32)[None])
    if mirrored:
        across = after(across, left_h, lower[2], lower[3])
        beside = swapped(jnp.concatenate([pivot_rows, across]), "row", 0)
        parts = [pivot_rows, across, beside]
        homes = [block_rows ^ bits for bits in (0, 2, 1, 3)]
        first = lax.dynamic_slice_in_dim(pivot_came, sibling, 1, 0)
    else:
        for number in range(len(spans)):
            send(number, came[-2] if number > 1 else pivot_came)
        pivot_rows = place_rows(
            lax.dynamic_slice_in_dim(child_update[0, :, 0], sibling, 1, 0),
            pivot_came,
            ((own_rows[:1], own_cols), (other_rows[:1], other_cols)),
            diag_rows[:1],
            on_diagonal(blocks[:1]),
        )
        mine = (jnp.arange(pivots) == position)[:, None, None, None]
        parts = [lax.psum(jnp.where(mine, pivot_rows, 0.0), subcubes)]
        homes = [jnp.arange(pivots, dtype=jnp.int32)]
        first = pivot_came
    right_h, right_l = solve_columns(parts, jnp.concatenate(homes), high, low)
    if mirrored:
        turned[0] = after(turned[0], left_h)
        turned += [lax.ppermute(part, ("row", "col"), pairs) for part in lower[2:4]]
        send(1, turned[0])
        right_h = after(right_h, turned[0])

    front = None
    groups = cols // SUB
    for start, end in ((0, groups // 2), (groups // 2, groups)):
        front = own_part(
            front,
            child_update,
            own,
            (own_rows, own_cols),
            diag_rows,
            on_diagonal(blocks),
            (left_h, left_l),
            (right_h, right_l),
            panel,
            start,
            end,
        )
        if mirrored:
            if start > 0:
                send(2, front)
                lower[4] = after(lower[4], front)
            front = after(front, turned[1]) if start == 0 else after(front, turned[2], lower[4])
    if mirrored:
        turned.append(lax.ppermute(lower[4], ("row", "col"), pairs))
    front = add_first(front, first, other_rows[:1], trailing_cols)

    def turned_tiles(front, parts, low, top):
        steps = [
            (j, g)
            for j in range(low, top)
            for g in range(groups)
            if j < min(rows, (g + 1) * (SUB // 2)) - 1
        ]
        alone = within == column_index
        entries = []
        for part in parts:
            mine = (*cuts[part], rows, sibling, steps)
            entries.append(turned_entry(turned[part], *mine, ~alone))
            entries.append(turned_entry(lower[part], *mine, alone))
        return add_tiles(front, entries, steps, other_rows, trailing_cols)

    for number, (at, count) in enumerate(spans):
        if len(came) < len(spans):
            send(len(came), front)
        flat = came[number].reshape(-1, tile, tile)
        steps = [(j, g) for j in range(at, at + count) for g in range(groups)]
        if mirrored:
            if number == 2:
                front = turned_tiles(after(front, turned[3]), (0, 1, 2), 1, near)
            if number == len(spans) - 1:
                front = turned_tiles(front, (3, 4), near, rows)
            entries = [cross_entry(flat, rows, 1 - sibling, steps)]
            for part, cut in zip(lower, cuts):
                entries.append(straight_entry(part, *cut, rows, sibling, steps))
        else:
            j, g = np.array(steps).T
            slot = np.arange(SUB)[:, None]
            picks = jnp.asarray((j - at) * cols + g * SUB + slot, jnp.int32)
            stands = jnp.asarray(np.broadcast_to(2 * slot, picks.shape), jnp.int32)
            entries = [(flat, picks, stands, np.ones(SUB, bool))]
        front = add_tiles(front, entries, steps, other_rows, trailing_cols)
    return front


def solution(mesh):
    return jax.shard_map(
        on_device,
        mesh=mesh,
        in_specs=(P(("cube", "row"), None, None, None, "col", None), P(), P()),
        out_specs=P(("cube", "row"), None, None, "col", None),
        check_vma=False,
    )
```

```python
import jax
import jax.numpy as jnp
import numpy as np
from jax import lax
from jax.experimental import pallas as pl
from jax.experimental.pallas import tpu as pltpu
from jax.sharding import PartitionSpec as P

K = 1024
F32 = jnp.float32
BF16 = jnp.bfloat16
SUB = 8
BATCH = 32
WEIGHT = 0.01
VMEM_LIMIT = 56 * 1024 * 1024


def params(steps=1):
    return pltpu.CompilerParams(
        dimension_semantics=("arbitrary",) * steps, vmem_limit_bytes=VMEM_LIMIT
    )


def cost(flops, moved):
    return pl.CostEstimate(
        flops=int(flops * WEIGHT), bytes_accessed=int(moved * WEIGHT), transcendentals=0
    )


def swapped(value, axis, distance):
    mask = 2**distance
    pairs = [(source, source ^ mask) for source in range(lax.axis_size(axis))]
    return lax.ppermute(value, axis, pairs)


def after(value, *others):
    return lax.optimization_barrier((value,) + others)[0]


def inverse_map(values, starts):
    tile = values.shape[-1]
    offsets = jnp.arange(tile, dtype=jnp.int32)
    hit = (values - starts[:, None])[:, None, :] == offsets[None, :, None]
    return jnp.sum(jnp.where(hit, offsets[None, None, :] + 1, 0), axis=-1).astype(jnp.int32) - 1


def split(value):
    high = value.astype(BF16)
    return high, (value - high.astype(F32)).astype(BF16)


def dot(a, b):
    return jnp.dot(a, b, preferred_element_type=F32)


def dot_nt(a, b):
    return lax.dot_general(a, b, (((1,), (1,)), ((), ())), preferred_element_type=F32)


def dot_full(a, b, dims):
    return lax.dot_general(
        a, b, (dims, ((), ())), precision=lax.Precision.HIGHEST, preferred_element_type=F32
    )


def pack_panel(child, half, count):
    _, _, rows, tile, _, lanes = child.shape
    block = min(4, rows)

    def kernel(half_ref, raw, out):
        flat = raw.reshape(block * tile * SUB, lanes)
        for b in range(block):
            for p in range(count):
                out[b, p] = flat[pl.ds(b * tile * SUB + p, tile, SUB), :]

    return pl.pallas_call(
        kernel,
        grid_spec=pltpu.PrefetchScalarGridSpec(
            num_scalar_prefetch=1,
            grid=(rows // block,),
            in_specs=[
                pl.BlockSpec((1, 1, block, tile, SUB, lanes), lambda j, h: (0, h[0], j, 0, 0, 0))
            ],
            out_specs=pl.BlockSpec((block, count, tile, lanes), lambda j, h: (j, 0, 0, 0)),
        ),
        out_shape=jax.ShapeDtypeStruct((rows, count, tile, lanes), F32),
        compiler_params=params(),
        cost_estimate=cost(0, rows * tile * lanes * 4 * (SUB + count)),
        name="pack_panel",
    )(half, child)


def pack_cross(child, half, parity):
    _, _, rows, tile, cols, lanes = child.shape
    pairs = cols // 2

    def kernel(half_ref, parity_ref, raw, out):
        for i in range(1, pairs):
            at = pl.ds(2 * i + parity_ref[0], tile, cols)
            out[0, i - 1] = raw.reshape(tile * cols, lanes)[at, :]

    return pl.pallas_call(
        kernel,
        grid_spec=pltpu.PrefetchScalarGridSpec(
            num_scalar_prefetch=2,
            grid=(rows - 1,),
            in_specs=[
                pl.BlockSpec(
                    (1, 1, 1, tile, cols, lanes), lambda j, h, b: (0, h[0], j + 1, 0, 0, 0)
                )
            ],
            out_specs=pl.BlockSpec((1, pairs - 1, tile, lanes), lambda j, h, b: (j, 0, 0, 0)),
        ),
        out_shape=jax.ShapeDtypeStruct((rows - 1, pairs - 1, tile, lanes), F32),
        compiler_params=params(),
        cost_estimate=cost(0, rows * tile * lanes * 4 * (cols + pairs)),
        name="pack_cross",
    )(half, parity, child)


def lower_start(row, first, last):
    width = last - first
    short, long = row - first, row - last
    return short * (short + 1) // 2 if long <= 0 else width * (width + 1) // 2 + long * width


def pack_lower(child, half, parity, first, last):
    _, _, rows, tile, cols, lanes = child.shape
    count = lower_start(rows, first, last)
    width = last - first

    def kernel(half_ref, parity_ref, raw, out):
        j = pl.program_id(0) + first
        short, long = j - first, j - last
        start = jnp.where(
            long <= 0, short * (short + 1) // 2, width * (width + 1) // 2 + long * width
        )
        flat = raw.reshape(tile * cols, lanes)
        for i in range(first, last):
            @pl.when(i <= j)
            def _():
                out[start + i - first] = flat[pl.ds(2 * i + parity_ref[0], tile, cols), :]

    return pl.pallas_call(
        kernel,
        grid_spec=pltpu.PrefetchScalarGridSpec(
            num_scalar_prefetch=2,
            grid=(rows - first,),
            in_specs=[
                pl.BlockSpec(
                    (1, 1, 1, tile, cols, lanes), lambda j, h, b: (0, h[0], j + first, 0, 0, 0)
                )
            ],
            out_specs=pl.BlockSpec((count, tile, lanes), lambda j, h, b: (0, 0, 0)),
        ),
        out_shape=jax.ShapeDtypeStruct((count, tile, lanes), F32),
        compiler_params=params(),
        cost_estimate=cost(0, tile * lanes * 4 * ((rows - first) * cols + count)),
        name="pack_lower",
    )(half, parity, child)


def pack_all(child, half):
    _, _, rows, tile, cols, lanes = child.shape

    def kernel(half_ref, raw, out):
        for p in range(cols):
            out[0, p] = raw.reshape(tile * cols, lanes)[pl.ds(p, tile, cols), :]

    return pl.pallas_call(
        kernel,
        grid_spec=pltpu.PrefetchScalarGridSpec(
            num_scalar_prefetch=1,
            grid=(rows - 1,),
            in_specs=[
                pl.BlockSpec((1, 1, 1, tile, cols, lanes), lambda j, h: (0, h[0], j + 1, 0, 0, 0))
            ],
            out_specs=pl.BlockSpec((1, cols, tile, lanes), lambda j, h: (j, 0, 0, 0)),
        ),
        out_shape=jax.ShapeDtypeStruct((rows - 1, cols, tile, lanes), F32),
        compiler_params=params(),
        cost_estimate=cost(0, rows * tile * lanes * 8 * cols),
        name="pack_all",
    )(half, child)


def place_block(rowmap, row, load, columns, store):
    tile = columns.shape[-1]
    live = columns >= 0
    lanes = jnp.maximum(columns, 0)

    def body(step, carry):
        index = [rowmap[row, step * BATCH + r] for r in range(BATCH)]
        values = [load(jnp.maximum(i, 0)) for i in index]
        values = [
            jnp.take_along_axis(v, lanes, axis=1, mode="promise_in_bounds") for v in values
        ]
        store(step * BATCH, [jnp.where(live & (i >= 0), v, 0.0) for i, v in zip(index, values)])
        return carry

    lax.fori_loop(0, tile // BATCH, body, 0)


def place_rows(first, second, maps, diag, where):
    count, tile, cols, lanes = first.shape
    (rows0, cols0), (rows1, cols1) = maps

    def kernel(rows0_ref, rows1_ref, where_ref, u0, u1, c0, c1, d, out, flat):
        n, g = pl.program_id(0), pl.program_id(1)

        def put(at, values):
            for r, value in enumerate(values):
                flat[pl.ds(pl.multiple_of((at + r) * SUB, SUB), SUB), :] = value

        def add(at, values):
            spots = [pl.ds(pl.multiple_of((at + r) * SUB, SUB), SUB) for r in range(BATCH)]
            values = [flat[spot, :] + value for spot, value in zip(spots, values)]
            for spot, value in zip(spots, values):
                flat[spot, :] = value

        place_block(rows0_ref, n, lambda s: u0[0, s], c0[...], put)
        place_block(rows1_ref, n, lambda s: u1[0, s], c1[...], add)
        for p in range(SUB):
            out[0, p] = flat[pl.ds(p, tile, SUB), :]

            @pl.when(where_ref[n] == g * SUB + p)
            def _():
                eye = lax.broadcasted_iota(jnp.int32, (tile, lanes), 0) == (
                    lax.broadcasted_iota(jnp.int32, (tile, lanes), 1)
                )
                out[0, p] += jnp.where(eye, d[0], 0.0)

    return pl.pallas_call(
        kernel,
        grid_spec=pltpu.PrefetchScalarGridSpec(
            num_scalar_prefetch=3,
            grid=(count, cols // SUB),
            in_specs=[
                pl.BlockSpec((1, tile, SUB, lanes), lambda n, g, *_: (n, 0, g, 0)),
                pl.BlockSpec((1, tile, SUB, lanes), lambda n, g, *_: (n, 0, g, 0)),
                pl.BlockSpec((SUB, lanes), lambda n, g, *_: (g, 0)),
                pl.BlockSpec((SUB, lanes), lambda n, g, *_: (g, 0)),
                pl.BlockSpec((1, 1, lanes), lambda n, g, *_: (n, 0, 0)),
            ],
            out_specs=pl.BlockSpec((1, SUB, tile, lanes), lambda n, g, *_: (n, g, 0, 0)),
            scratch_shapes=[pltpu.VMEM((tile * SUB, lanes), F32)],
        ),
        out_shape=jax.ShapeDtypeStruct((count, cols, tile, lanes), F32),
        compiler_params=params(2),
        cost_estimate=cost(0, count * cols * tile * lanes * 12),
        name="place_rows",
    )(rows0, rows1, where, first, second, cols0, cols1, diag[:, None, :])


def eliminate(block):
    tile = block.shape[0]
    lane = lax.broadcasted_iota(jnp.int32, (1, tile), 1)
    sub = lax.broadcasted_iota(jnp.int32, (tile, 1), 0)

    def at_lane(value, j):
        index = jnp.full(value.shape, j, jnp.int32)
        return jnp.take_along_axis(value, index, axis=1, mode="promise_in_bounds")

    def body(g, carry):
        at = pl.multiple_of(g * SUB, SUB)
        rows = block[pl.ds(at, SUB), :]
        whole = block[...].reshape(tile // SUB, SUB, tile)
        within = lax.broadcasted_iota(jnp.int32, (SUB, tile), 0)
        below = sub.reshape(tile // SUB, SUB, 1) >= at + SUB
        for r in range(SUB):
            j = at + r
            here = lane == j
            row = jnp.broadcast_to(rows[r : r + 1, :], (SUB, tile))
            pivot = at_lane(row, j)
            root = lax.rsqrt(pivot)
            root = root * (1.5 - 0.5 * pivot * root * root)
            row = jnp.where(here, root, row * root)
            column = at_lane(rows, j) * root
            under = within > r
            rows = jnp.where(
                under,
                jnp.where(here, 0.0, rows) - column * row,
                jnp.where(within == r, row, rows),
            )
            column = at_lane(whole.reshape(tile, tile), j).reshape(whole.shape) * root[None]
            whole = jnp.where(here[None], 0.0, whole) - column * row[None]
        block[...] = jnp.where(below, whole, block[...].reshape(whole.shape)).reshape(tile, tile)
        block[pl.ds(at, SUB), :] = rows
        return carry

    lax.fori_loop(0, tile // SUB, body, 0)
    low = lax.broadcasted_iota(jnp.int32, (tile, tile), 0) >= (
        lax.broadcasted_iota(jnp.int32, (tile, tile), 1)
    )
    return jnp.where(low, block[...], 0.0)


def inverse_factor(pivot, tile):
    order = pivot.shape[0]
    steps = order // tile

    def kernel(a, high, low, m, block):
        m[...] = a[...]
        for s in range(steps):
            top, end = s * tile, (s + 1) * tile
            block[...] = m[top:end, top:end]
            inverse = eliminate(block)
            strip = dot_full(inverse, m[top:end, :], ((1,), (0,)))
            pieces = [strip[:, :top]] if top > 0 else []
            pieces += [inverse] + ([strip[:, end:]] if end < order else [])
            strip = jnp.concatenate(pieces, axis=1)
            if end < order:
                m[end:, top:end] = jnp.zeros((order - end, tile), F32)
                m[end:, :] -= dot_full(strip[:, end:], strip, ((0,), (0,)))
                m[top:end, end:] = jnp.zeros((tile, order - end), F32)
            m[top:end, :end] = strip[:, :end]
        head, tail = split(m[...])
        high[...] = head
        low[...] = tail

    return pl.pallas_call(
        kernel,
        in_specs=[pl.BlockSpec(memory_space=pltpu.VMEM)],
        out_specs=[pl.BlockSpec(memory_space=pltpu.VMEM)] * 2,
        out_shape=[jax.ShapeDtypeStruct((order, order), BF16)] * 2,
        scratch_shapes=[pltpu.VMEM((order, order), F32), pltpu.VMEM((tile, tile), F32)],
        compiler_params=pltpu.CompilerParams(vmem_limit_bytes=VMEM_LIMIT),
        cost_estimate=cost(100e9, order * order * 8),
        name="inverse_factor",
    )(pivot)


def solve_rows(gathered, high, low, column_index):
    columns, rows, local = gathered.shape
    order = high.shape[0]
    tile = 128
    pieces = local // tile
    step = 256

    def kernel(me, f, h, l, out_h, out_l, out_f, acc):
        total = jnp.zeros((step, order), F32)
        for c in range(columns):
            fh, fl = split(f[c])
            spans = [
                slice((n * columns + c) * tile, (n * columns + c + 1) * tile) for n in range(pieces)
            ]
            gh = jnp.concatenate([h[:, s] for s in spans], axis=1)
            gl = jnp.concatenate([l[:, s] for s in spans], axis=1)
            total += dot_nt(fh, gh) + (dot_nt(fh, gl) + dot_nt(fl, gh))
        acc[...] = total
        xh, xl = split(total)
        out_h[...] = xh
        out_l[...] = xl
        for n in range(pieces):
            at = pl.multiple_of((n * columns + me[0]) * tile, tile)
            out_f[n] = acc[:, pl.ds(at, tile)]

    return pl.pallas_call(
        kernel,
        grid_spec=pltpu.PrefetchScalarGridSpec(
            num_scalar_prefetch=1,
            grid=(rows // step,),
            in_specs=[
                pl.BlockSpec((columns, step, local), lambda r, *_: (0, r, 0)),
                pl.BlockSpec((order, order), lambda r, *_: (0, 0)),
                pl.BlockSpec((order, order), lambda r, *_: (0, 0)),
            ],
            out_specs=[
                pl.BlockSpec((step, order), lambda r, *_: (r, 0)),
                pl.BlockSpec((step, order), lambda r, *_: (r, 0)),
                pl.BlockSpec((pieces, step, tile), lambda r, *_: (0, r, 0)),
            ],
            scratch_shapes=[pltpu.VMEM((step, order), F32)],
        ),
        out_shape=[
            jax.ShapeDtypeStruct((rows, order), BF16),
            jax.ShapeDtypeStruct((rows, order), BF16),
            jax.ShapeDtypeStruct((pieces, rows, tile), F32),
        ],
        compiler_params=params(),
        cost_estimate=cost(6 * rows * order * order, rows * order * 8),
        name="solve_rows",
    )(column_index, gathered, high, low)


def solve_columns(parts, homes, high, low):
    _, cols, tile, lanes = parts[0].shape
    order = high.shape[0]
    wide = 4
    deep = 256
    width = len(parts)

    def kernel(home, *refs):
        f, (h, l, out_h, out_l, fh, fl) = refs[:width], refs[width:]
        number = 0
        for part in f:
            for b in range(part.shape[0]):
                block = jnp.concatenate([part[b, p] for p in range(wide)], axis=1)
                rows = pl.ds(pl.multiple_of(home[number] * tile, tile), tile)
                fh[rows, :], fl[rows, :] = split(block)
                number += 1
        for r in range(order // deep):
            span, depth = slice(r * deep, (r + 1) * deep), (r + 1) * deep
            lh, ll = h[span, :depth], l[span, :depth]
            x = dot(lh, fh[:depth]) + (dot(lh, fl[:depth]) + dot(ll, fh[:depth]))
            out_h[span, :], out_l[span, :] = split(x)

    return pl.pallas_call(
        kernel,
        grid_spec=pltpu.PrefetchScalarGridSpec(
            num_scalar_prefetch=1,
            grid=(cols // wide,),
            in_specs=[
                pl.BlockSpec((part.shape[0], wide, tile, lanes), lambda g, *_: (0, g, 0, 0))
                for part in parts
            ]
            + [pl.BlockSpec((order, order), lambda g, *_: (0, 0))] * 2,
            out_specs=[pl.BlockSpec((order, wide * lanes), lambda g, *_: (0, g))] * 2,
            scratch_shapes=[pltpu.VMEM((order, wide * lanes), BF16)] * 2,
        ),
        out_shape=[jax.ShapeDtypeStruct((order, cols * lanes), BF16)] * 2,
        compiler_params=params(),
        cost_estimate=cost(4 * order * order * cols * lanes, order * cols * lanes * 8),
        name="solve_columns",
    )(homes, *parts, high, low)


def own_part(before, child, half, own_maps, diag, where, left, right, panel, start, end):
    _, _, rows, tile, cols, lanes = child.shape
    rowmap, colmap = own_maps
    xh, xl = left
    ch, cl = right
    order = xh.shape[1]
    count = panel.shape[0]
    block = min(4, rows)

    def kernel(half_ref, map_ref, where_ref, *refs):
        u, c, d, lh, ll, rh, rl, pan, out, flat = refs[-10:]
        g, n = pl.program_id(0) + start, pl.program_id(1)
        columns = c[...]
        for b in range(block):
            j = n * block + b

            def put(at, values):
                for r, value in enumerate(values):
                    spot = pl.multiple_of((b * tile + at + r) * SUB, SUB)
                    flat[pl.ds(spot, SUB), :] = value

            place_block(map_ref, j, lambda s: u[0, 0, b, s], columns, put)
            for p in range(SUB):
                @pl.when(where_ref[j] == g * SUB + p)
                def _():
                    eye = lax.broadcasted_iota(jnp.int32, (tile, lanes), 0) == (
                        lax.broadcasted_iota(jnp.int32, (tile, lanes), 1)
                    )
                    flat[pl.ds(b * tile * SUB + p, tile, SUB), :] += jnp.where(eye, d[b], 0.0)
        lhs_h, lhs_l = lh[...], ll[...]
        for pair in range(SUB // 2):
            span = slice(pair * 2 * lanes, (pair + 1) * 2 * lanes)
            update = dot(lhs_h, rh[:, span]) + (dot(lhs_h, rl[:, span]) + dot(lhs_l, rh[:, span]))
            for b in range(block):
                for side in range(2):
                    at = pl.ds(b * tile * SUB + 2 * pair + side, tile, SUB)
                    part = update[b * tile : (b + 1) * tile, side * lanes : (side + 1) * lanes]
                    flat[at, :] -= part

        @pl.when(g == 0)
        def _():
            for b in range(block):
                for p in range(count):
                    flat[pl.ds(b * tile * SUB + p, tile, SUB), :] = pan[
                        p, b * tile : (b + 1) * tile, :
                    ]

        out[...] = flat[...].reshape(out.shape)

    held = [] if before is None else [pl.BlockSpec(memory_space=pl.ANY)]
    return pl.pallas_call(
        kernel,
        grid_spec=pltpu.PrefetchScalarGridSpec(
            num_scalar_prefetch=3,
            grid=(end - start, rows // block),
            in_specs=held
            + [
                pl.BlockSpec(
                    (1, 1, block, tile, SUB, lanes), lambda g, n, h, *_: (0, h[0], n, 0, g + start, 0)
                ),
                pl.BlockSpec((SUB, lanes), lambda g, n, *_: (g + start, 0)),
                pl.BlockSpec((block, 1, lanes), lambda g, n, *_: (n, 0, 0)),
                pl.BlockSpec((block * tile, order), lambda g, n, *_: (n, 0)),
                pl.BlockSpec((block * tile, order), lambda g, n, *_: (n, 0)),
                pl.BlockSpec((order, SUB * lanes), lambda g, n, *_: (0, g + start)),
                pl.BlockSpec((order, SUB * lanes), lambda g, n, *_: (0, g + start)),
                pl.BlockSpec((count, block * tile, lanes), lambda g, n, *_: (0, n, 0)),
            ],
            out_specs=pl.BlockSpec((1, block, tile, SUB, lanes), lambda g, n, *_: (0, n, 0, g + start, 0)),
            scratch_shapes=[pltpu.VMEM((block * tile * SUB, lanes), F32)],
        ),
        out_shape=jax.ShapeDtypeStruct((1, rows, tile, cols, lanes), F32),
        input_output_aliases={} if before is None else {3: 0},
        compiler_params=params(2),
        cost_estimate=cost(
            6 * rows * tile * order * cols * lanes, rows * tile * cols * lanes * 8
        ),
        name="own_part",
    )(half, rowmap, where, *([] if before is None else [before]), child, colmap, diag[:, None, :], xh, xl, ch, cl, panel)


def add_first(front, block, rowmap, colmap):
    _, _, tile, cols, lanes = front.shape

    def kernel(map_ref, before, u, c, out):
        def add(at, values):
            values = [before[0, 0, at + r] + value for r, value in enumerate(values)]
            for r, value in enumerate(values):
                out[0, 0, at + r] = value

        place_block(map_ref, 0, lambda s: u[0, s], c[...], add)

    spec = pl.BlockSpec((1, 1, tile, SUB, lanes), lambda g, *_: (0, 0, 0, g, 0))
    return pl.pallas_call(
        kernel,
        grid_spec=pltpu.PrefetchScalarGridSpec(
            num_scalar_prefetch=1,
            grid=(cols // SUB,),
            in_specs=[
                spec,
                pl.BlockSpec((1, tile, SUB, lanes), lambda g, *_: (0, 0, g, 0)),
                pl.BlockSpec((SUB, lanes), lambda g, *_: (g, 0)),
            ],
            out_specs=spec,
        ),
        out_shape=jax.ShapeDtypeStruct(front.shape, F32),
        input_output_aliases={1: 0},
        compiler_params=params(),
        cost_estimate=cost(0, tile * cols * lanes * 12),
        name="add_first",
    )(rowmap, front, block, colmap)


def add_tiles(front, entries, steps, rowmap, colmap):
    _, _, tile, cols, lanes = front.shape
    sources, picks, stands = [], [], []
    for array, pick, stand, ever in entries:
        for slot in range(len(ever)):
            if ever[slot]:
                sources.append(array)
                picks.append(pick[slot])
                stands.append(stand[slot])
    width, count = len(sources), len(steps)
    picks, stands = (jnp.concatenate(t).astype(jnp.int32) for t in (picks, stands))
    order = jnp.array([row for row, _ in steps] + [group for _, group in steps], jnp.int32)

    def kernel(map_ref, order_ref, picks_ref, stands_ref, before, *refs):
        tiles, (c, out, flat) = refs[:width], refs[width:]
        n = pl.program_id(0)
        sub = lax.broadcasted_iota(jnp.int32, (SUB, lanes), 0)
        given = jnp.zeros((SUB, lanes), jnp.int32)
        for slot in range(width):
            stand = stands_ref[slot * count + n]
            p = stand // 2
            given = jnp.where((stand >= 0) & (sub == p), 1, given)

            @pl.when((stand >= 0) & (stand % 2 == 0))
            def _():
                flat[pl.ds(p, tile, SUB), :] = tiles[slot][0]

            @pl.when((stand >= 0) & (stand % 2 == 1))
            def _():
                flat[pl.ds(p, tile, SUB), :] = tiles[slot][0].T

        def load(source):
            return flat[pl.ds(pl.multiple_of(source * SUB, SUB), SUB), :]

        def add(at, values):
            values = [before[0, 0, at + r] + value for r, value in enumerate(values)]
            for r, value in enumerate(values):
                out[0, 0, at + r] = value

        place_block(map_ref, order_ref[n], load, jnp.where(given == 1, c[...], -1), add)

    spec = pl.BlockSpec(
        (1, 1, tile, SUB, lanes), lambda n, m, o, *_: (0, o[n], 0, o[count + n], 0)
    )

    def tile_spec(slot):
        return pl.BlockSpec((1, tile, lanes), lambda n, m, o, k, t: (k[slot * count + n], 0, 0))

    return pl.pallas_call(
        kernel,
        grid_spec=pltpu.PrefetchScalarGridSpec(
            num_scalar_prefetch=4,
            grid=(count,),
            in_specs=[spec]
            + [tile_spec(slot) for slot in range(width)]
            + [pl.BlockSpec((SUB, lanes), lambda n, m, o, *_: (o[count + n], 0))],
            out_specs=spec,
            scratch_shapes=[pltpu.VMEM((tile * SUB, lanes), F32)],
        ),
        out_shape=jax.ShapeDtypeStruct(front.shape, F32),
        input_output_aliases={4: 0},
        compiler_params=params(),
        cost_estimate=cost(0, count * tile * SUB * lanes * 12),
        name="add_tiles",
    )(rowmap, order, picks, stands, front, *sources, colmap)


def held_picks(picks, given):
    held = np.where(given, picks, 0)
    for step in range(1, held.shape[1]):
        held[:, step] = np.where(given[:, step], held[:, step], held[:, step - 1])
    return held.astype(np.int32)


def straight_entry(array, first, last, rows, parity, steps):
    j, g = np.array(steps).T
    i = g[None, :] * (SUB // 2) + np.arange(SUB // 2)[:, None]
    begins = np.array([lower_start(max(row, first), first, last) for row in range(rows)])
    given = (i >= first) & (i < last) & (i <= j)
    picks = held_picks(begins[j] + i - first, given)
    place = 2 * (2 * np.arange(SUB // 2)[:, None] + parity)
    return array, jnp.asarray(picks), jnp.where(given, place, -1), given.any(axis=1)


def turned_entry(array, first, last, rows, parity, steps, used):
    j, g = np.array(steps).T
    i = g[None, :] * (SUB // 2) + np.arange(SUB // 2)[:, None]
    begins = np.array([lower_start(max(row, first), first, last) for row in range(rows)])
    given = (j >= first) & (j < last) & (i > j)
    picks = held_picks(begins[i] + j - first, given)
    place = 2 * (2 * np.arange(SUB // 2)[:, None] + parity) + 1
    stands = jnp.where(given & used, place, -1)
    return array, jnp.where(used, picks, 0), stands, given.any(axis=1)


def cross_entry(array, rows, parity, steps):
    j, g = np.array(steps).T
    i = g[None, :] * (SUB // 2) + np.arange(SUB // 2)[:, None]
    given = i >= 1
    picks = held_picks((j - j[0]) * (rows - 1) + i - 1, given)
    place = 2 * (2 * np.arange(SUB // 2)[:, None] + parity)
    return array, jnp.asarray(picks), jnp.where(given, place, -1), given.any(axis=1)


def on_device(child_update, child_map, parent_diag):
    grid_size = lax.axis_size(("cube", "row"))
    half_grid = grid_size // 2
    columns = lax.axis_size("col")
    position = lax.axis_index(("cube", "row"))
    column_index = lax.axis_index("col")
    sibling = position // half_grid
    within = position % half_grid
    _, _, rows, tile, cols, lanes = child_update.shape
    distance = half_grid.bit_length() - 1
    pivots = K // tile
    local = pivots // columns
    mirrored = (
        grid_size == pivots
        and half_grid == columns
        and lax.axis_size("row") == half_grid
        and cols == 2 * rows
    )
    own = sibling.astype(jnp.int32)[None]
    other = 1 - own

    starts = tile * jnp.arange(rows * grid_size, dtype=jnp.int32)
    sources = jnp.stack(
        [inverse_map(child_map[e].reshape(-1, tile), starts) for e in range(2)]
    )

    def row_maps(child):
        of = lax.dynamic_index_in_dim(sources, child, 0, keepdims=False)
        of = of.reshape(rows, 2, half_grid, tile)
        return lax.dynamic_index_in_dim(of, within, 2, keepdims=False)

    def col_maps(child):
        of = lax.dynamic_index_in_dim(sources, child, 0, keepdims=False)
        of = of.reshape(cols, columns, tile)
        return lax.dynamic_index_in_dim(of, column_index, 1, keepdims=False)

    own_halves, other_halves = row_maps(sibling), row_maps(1 - sibling)
    own_cols, other_cols = col_maps(sibling), col_maps(1 - sibling)
    own_rows = lax.dynamic_index_in_dim(own_halves, sibling, 1, keepdims=False)
    other_rows = lax.dynamic_index_in_dim(other_halves, sibling, 1, keepdims=False)
    trailing_cols = jnp.where(jnp.arange(cols)[:, None] < local, -1, other_cols)

    blocks = grid_size * jnp.arange(rows, dtype=jnp.int32) + position
    diag_tiles = parent_diag.reshape(-1, tile)

    def on_diagonal(block_rows):
        offset = block_rows - column_index
        return jnp.where(offset % columns == 0, offset // columns, -1).astype(jnp.int32)

    diag_rows = diag_tiles[blocks]

    subcubes = ("cube", "row")
    spans, at = [], 1
    while at < rows:
        count = -(-3 * (rows - at) // 10)
        spans.append((at, count))
        at += count

    panel_sent = pack_panel(child_update, other, local)
    panel_own = pack_panel(after(child_update, panel_sent), own, local)
    panel_came = swapped(panel_sent, subcubes, distance)
    if mirrored:
        near = spans[0][0] + spans[0][1]
        edges = [1, 2, 4, near, near + 2, rows]
        cuts = list(zip(edges[:-1], edges[1:]))
        lower_sent = [pack_lower(child_update, other, other, a, b) for a, b in cuts]
        pivot_sent = after(child_update, panel_sent)[0, :, 0]
        panel_came = after(panel_came, panel_own, pivot_sent, *lower_sent[:3])
    else:
        pivot_sent = lax.dynamic_slice_in_dim(child_update[0, :, 0], 1 - sibling, 1, 0)

    def placed(tiles, row_map, col_map):
        offsets = jnp.arange(tile, dtype=jnp.int32)
        row_hot = (row_map[:, :, None] == offsets).astype(F32)
        col_hot = (col_map[:local, :, None] == offsets).astype(F32)
        done = jnp.einsum("jos,jpsv->jpov", row_hot, tiles, precision=lax.Precision.HIGHEST)
        return jnp.einsum("jpov,pqv->jopq", done, col_hot, precision=lax.Precision.HIGHEST)

    hits = on_diagonal(blocks)[:, None] == jnp.arange(local)
    eye = jnp.eye(tile, dtype=bool)[None, :, None, :] & hits[:, None, :, None]
    front_panel = placed(panel_own, own_rows, own_cols)
    front_panel += placed(panel_came, other_rows, other_cols)
    front_panel += jnp.where(eye, diag_rows[:, :, None, None], 0.0)

    pivot = lax.all_gather(front_panel[0], ("cube", "row", "col"), axis=0, tiled=False)
    gathered = lax.all_gather(
        front_panel.reshape(rows * tile, local * tile), "col", axis=0, tiled=False
    )
    pivot = pivot.reshape(grid_size, columns, tile, local, tile)[:pivots]
    pivot = jnp.transpose(pivot, (0, 2, 3, 1, 4)).reshape(K, K)

    pivot_came = swapped(pivot_sent, subcubes, distance)
    if mirrored:
        pairs = [
            (r * columns + c, c * columns + r)
            for r in range(half_grid)
            for c in range(columns)
            if r != c
        ]
        lower = [swapped(after(part, front_panel), subcubes, distance) for part in lower_sent[:3]]
        sent = pack_cross(after(child_update, front_panel), other, own)
        pivot_came = after(pivot_came, sent, *lower_sent[3:])
        lower += [swapped(after(part, pivot_came), subcubes, distance) for part in lower_sent[3:]]
        block_rows = half_grid * jnp.arange(2, dtype=jnp.int32) + within
        pivot_rows = place_rows(
            pivot_sent,
            pivot_came,
            ((own_halves[0], own_cols), (other_halves[0], other_cols)),
            diag_tiles[block_rows],
            on_diagonal(block_rows),
        )
        across = swapped(pivot_rows, "row", 1)
        pivot = after(pivot, pivot_rows)
    else:
        sent = pack_all(child_update, other)
    high, low = inverse_factor(pivot, tile)

    came = []

    def send(number, behind):
        at, count = spans[number]
        part = after(sent[at - 1 : at - 1 + count], behind)
        came.append(swapped(part, subcubes, distance))

    if mirrored:
        lower[:2] = [after(part, high) for part in lower[:2]]
        turned = [lax.ppermute(part, ("row", "col"), pairs) for part in lower[:2]]
        send(0, lower[1])
        gathered = after(gathered, *lower[:2])
    left_h, left_l, panel = solve_rows(gathered, high, low, column_index.astype(jnp.int32)[None])
    if mirrored:
        across = after(across, left_h, lower[2], lower[3])
        beside = swapped(jnp.concatenate([pivot_rows, across]), "row", 0)
        parts = [pivot_rows, across, beside]
        homes = [block_rows ^ bits for bits in (0, 2, 1, 3)]
        first = lax.dynamic_slice_in_dim(pivot_came, sibling, 1, 0)
    else:
        for number in range(len(spans)):
            send(number, came[-2] if number > 1 else pivot_came)
        pivot_rows = place_rows(
            lax.dynamic_slice_in_dim(child_update[0, :, 0], sibling, 1, 0),
            pivot_came,
            ((own_rows[:1], own_cols), (other_rows[:1], other_cols)),
            diag_rows[:1],
            on_diagonal(blocks[:1]),
        )
        mine = (jnp.arange(pivots) == position)[:, None, None, None]
        parts = [lax.psum(jnp.where(mine, pivot_rows, 0.0), subcubes)]
        homes = [jnp.arange(pivots, dtype=jnp.int32)]
        first = pivot_came
    right_h, right_l = solve_columns(parts, jnp.concatenate(homes), high, low)
    if mirrored:
        turned += [lax.ppermute(part, ("row", "col"), pairs) for part in lower[2:4]]

    front = None
    groups = cols // SUB
    for start, end in ((0, groups // 2), (groups // 2, groups)):
        front = own_part(
            front,
            child_update,
            own,
            (own_rows, own_cols),
            diag_rows,
            on_diagonal(blocks),
            (left_h, left_l),
            (right_h, right_l),
            panel,
            start,
            end,
        )
        if mirrored:
            if start == 0:
                turned[0] = after(turned[0], front)
                send(1, turned[0])
                front = after(front, turned[0])
            else:
                send(2, front)
                lower[4] = after(lower[4], front)
                front = after(front, turned[1], turned[2], lower[4])
    if mirrored:
        turned.append(lax.ppermute(lower[4], ("row", "col"), pairs))
    front = add_first(front, first, other_rows[:1], trailing_cols)

    def turned_tiles(front, parts, low, top):
        steps = [
            (j, g)
            for j in range(low, top)
            for g in range(groups)
            if j < min(rows, (g + 1) * (SUB // 2)) - 1
        ]
        alone = within == column_index
        entries = []
        for part in parts:
            mine = (*cuts[part], rows, sibling, steps)
            entries.append(turned_entry(turned[part], *mine, ~alone))
            entries.append(turned_entry(lower[part], *mine, alone))
        return add_tiles(front, entries, steps, other_rows, trailing_cols)

    for number, (at, count) in enumerate(spans):
        if len(came) < len(spans):
            send(len(came), front)
        flat = came[number].reshape(-1, tile, tile)
        steps = [(j, g) for j in range(at, at + count) for g in range(groups)]
        if mirrored:
            if number == 2:
                front = turned_tiles(after(front, turned[3]), (0, 1, 2), 1, near)
            if number == len(spans) - 1:
                front = turned_tiles(front, (3, 4), near, rows)
            entries = [cross_entry(flat, rows, 1 - sibling, steps)]
            for part, cut in zip(lower, cuts):
                entries.append(straight_entry(part, *cut, rows, sibling, steps))
        else:
            j, g = np.array(steps).T
            slot = np.arange(SUB)[:, None]
            picks = jnp.asarray((j - at) * cols + g * SUB + slot, jnp.int32)
            stands = jnp.asarray(np.broadcast_to(2 * slot, picks.shape), jnp.int32)
            entries = [(flat, picks, stands, np.ones(SUB, bool))]
        front = add_tiles(front, entries, steps, other_rows, trailing_cols)
    return front


def solution(mesh):
    return jax.shard_map(
        on_device,
        mesh=mesh,
        in_specs=(P(("cube", "row"), None, None, None, "col", None), P(), P()),
        out_specs=P(("cube", "row"), None, None, "col", None),
        check_vma=False,
    )
```

```python
import jax
import jax.numpy as jnp
import numpy as np
from jax import lax
from jax.experimental import pallas as pl
from jax.experimental.pallas import tpu as pltpu
from jax.sharding import PartitionSpec as P

K = 1024
F32 = jnp.float32
BF16 = jnp.bfloat16
SUB = 8
BATCH = 32
WEIGHT = 0.01
VMEM_LIMIT = 56 * 1024 * 1024


def params(steps=1):
    return pltpu.CompilerParams(
        dimension_semantics=("arbitrary",) * steps, vmem_limit_bytes=VMEM_LIMIT
    )


def cost(flops, moved):
    return pl.CostEstimate(
        flops=int(flops * WEIGHT), bytes_accessed=int(moved * WEIGHT), transcendentals=0
    )


def swapped(value, axis, distance):
    mask = 2**distance
    pairs = [(source, source ^ mask) for source in range(lax.axis_size(axis))]
    return lax.ppermute(value, axis, pairs)


def after(value, *others):
    return lax.optimization_barrier((value,) + others)[0]


def inverse_map(values, starts):
    tile = values.shape[-1]
    offsets = jnp.arange(tile, dtype=jnp.int32)
    hit = (values - starts[:, None])[:, None, :] == offsets[None, :, None]
    return jnp.sum(jnp.where(hit, offsets[None, None, :] + 1, 0), axis=-1).astype(jnp.int32) - 1


def split(value):
    high = value.astype(BF16)
    return high, (value - high.astype(F32)).astype(BF16)


def dot(a, b):
    return jnp.dot(a, b, preferred_element_type=F32)


def dot_nt(a, b):
    return lax.dot_general(a, b, (((1,), (1,)), ((), ())), preferred_element_type=F32)


def dot_full(a, b, dims):
    return lax.dot_general(
        a, b, (dims, ((), ())), precision=lax.Precision.HIGHEST, preferred_element_type=F32
    )


def pack_panel(child, half, count):
    _, _, rows, tile, _, lanes = child.shape
    block = min(4, rows)

    def kernel(half_ref, raw, out):
        flat = raw.reshape(block * tile * SUB, lanes)
        for b in range(block):
            for p in range(count):
                out[b, p] = flat[pl.ds(b * tile * SUB + p, tile, SUB), :]

    return pl.pallas_call(
        kernel,
        grid_spec=pltpu.PrefetchScalarGridSpec(
            num_scalar_prefetch=1,
            grid=(rows // block,),
            in_specs=[
                pl.BlockSpec((1, 1, block, tile, SUB, lanes), lambda j, h: (0, h[0], j, 0, 0, 0))
            ],
            out_specs=pl.BlockSpec((block, count, tile, lanes), lambda j, h: (j, 0, 0, 0)),
        ),
        out_shape=jax.ShapeDtypeStruct((rows, count, tile, lanes), F32),
        compiler_params=params(),
        cost_estimate=cost(0, rows * tile * lanes * 4 * (SUB + count)),
        name="pack_panel",
    )(half, child)


def pack_cross(child, half, parity):
    _, _, rows, tile, cols, lanes = child.shape
    pairs = cols // 2

    def kernel(half_ref, parity_ref, raw, out):
        for i in range(1, pairs):
            at = pl.ds(2 * i + parity_ref[0], tile, cols)
            out[0, i - 1] = raw.reshape(tile * cols, lanes)[at, :]

    return pl.pallas_call(
        kernel,
        grid_spec=pltpu.PrefetchScalarGridSpec(
            num_scalar_prefetch=2,
            grid=(rows - 1,),
            in_specs=[
                pl.BlockSpec(
                    (1, 1, 1, tile, cols, lanes), lambda j, h, b: (0, h[0], j + 1, 0, 0, 0)
                )
            ],
            out_specs=pl.BlockSpec((1, pairs - 1, tile, lanes), lambda j, h, b: (j, 0, 0, 0)),
        ),
        out_shape=jax.ShapeDtypeStruct((rows - 1, pairs - 1, tile, lanes), F32),
        compiler_params=params(),
        cost_estimate=cost(0, rows * tile * lanes * 4 * (cols + pairs)),
        name="pack_cross",
    )(half, parity, child)


def lower_start(row, first, last):
    width = last - first
    short, long = row - first, row - last
    return short * (short + 1) // 2 if long <= 0 else width * (width + 1) // 2 + long * width


def pack_lower(child, half, parity, first, last):
    _, _, rows, tile, cols, lanes = child.shape
    count = lower_start(rows, first, last)
    width = last - first

    def kernel(half_ref, parity_ref, raw, out):
        j = pl.program_id(0) + first
        short, long = j - first, j - last
        start = jnp.where(
            long <= 0, short * (short + 1) // 2, width * (width + 1) // 2 + long * width
        )
        flat = raw.reshape(tile * cols, lanes)
        for i in range(first, last):
            @pl.when(i <= j)
            def _():
                out[start + i - first] = flat[pl.ds(2 * i + parity_ref[0], tile, cols), :]

    return pl.pallas_call(
        kernel,
        grid_spec=pltpu.PrefetchScalarGridSpec(
            num_scalar_prefetch=2,
            grid=(rows - first,),
            in_specs=[
                pl.BlockSpec(
                    (1, 1, 1, tile, cols, lanes), lambda j, h, b: (0, h[0], j + first, 0, 0, 0)
                )
            ],
            out_specs=pl.BlockSpec((count, tile, lanes), lambda j, h, b: (0, 0, 0)),
        ),
        out_shape=jax.ShapeDtypeStruct((count, tile, lanes), F32),
        compiler_params=params(),
        cost_estimate=cost(0, tile * lanes * 4 * ((rows - first) * cols + count)),
        name="pack_lower",
    )(half, parity, child)


def pack_all(child, half):
    _, _, rows, tile, cols, lanes = child.shape

    def kernel(half_ref, raw, out):
        for p in range(cols):
            out[0, p] = raw.reshape(tile * cols, lanes)[pl.ds(p, tile, cols), :]

    return pl.pallas_call(
        kernel,
        grid_spec=pltpu.PrefetchScalarGridSpec(
            num_scalar_prefetch=1,
            grid=(rows - 1,),
            in_specs=[
                pl.BlockSpec((1, 1, 1, tile, cols, lanes), lambda j, h: (0, h[0], j + 1, 0, 0, 0))
            ],
            out_specs=pl.BlockSpec((1, cols, tile, lanes), lambda j, h: (j, 0, 0, 0)),
        ),
        out_shape=jax.ShapeDtypeStruct((rows - 1, cols, tile, lanes), F32),
        compiler_params=params(),
        cost_estimate=cost(0, rows * tile * lanes * 8 * cols),
        name="pack_all",
    )(half, child)


def place_block(rowmap, row, load, columns, store):
    tile = columns.shape[-1]
    live = columns >= 0
    lanes = jnp.maximum(columns, 0)

    def body(step, carry):
        index = [rowmap[row, step * BATCH + r] for r in range(BATCH)]
        values = [load(jnp.maximum(i, 0)) for i in index]
        values = [
            jnp.take_along_axis(v, lanes, axis=1, mode="promise_in_bounds") for v in values
        ]
        store(step * BATCH, [jnp.where(live & (i >= 0), v, 0.0) for i, v in zip(index, values)])
        return carry

    lax.fori_loop(0, tile // BATCH, body, 0)


def place_rows(first, second, maps, diag, where):
    count, tile, cols, lanes = first.shape
    (rows0, cols0), (rows1, cols1) = maps

    def kernel(rows0_ref, rows1_ref, where_ref, u0, u1, c0, c1, d, out, flat):
        n, g = pl.program_id(0), pl.program_id(1)

        def put(at, values):
            for r, value in enumerate(values):
                flat[pl.ds(pl.multiple_of((at + r) * SUB, SUB), SUB), :] = value

        def add(at, values):
            spots = [pl.ds(pl.multiple_of((at + r) * SUB, SUB), SUB) for r in range(BATCH)]
            values = [flat[spot, :] + value for spot, value in zip(spots, values)]
            for spot, value in zip(spots, values):
                flat[spot, :] = value

        place_block(rows0_ref, n, lambda s: u0[0, s], c0[...], put)
        place_block(rows1_ref, n, lambda s: u1[0, s], c1[...], add)
        for p in range(SUB):
            out[0, p] = flat[pl.ds(p, tile, SUB), :]

            @pl.when(where_ref[n] == g * SUB + p)
            def _():
                eye = lax.broadcasted_iota(jnp.int32, (tile, lanes), 0) == (
                    lax.broadcasted_iota(jnp.int32, (tile, lanes), 1)
                )
                out[0, p] += jnp.where(eye, d[0], 0.0)

    return pl.pallas_call(
        kernel,
        grid_spec=pltpu.PrefetchScalarGridSpec(
            num_scalar_prefetch=3,
            grid=(count, cols // SUB),
            in_specs=[
                pl.BlockSpec((1, tile, SUB, lanes), lambda n, g, *_: (n, 0, g, 0)),
                pl.BlockSpec((1, tile, SUB, lanes), lambda n, g, *_: (n, 0, g, 0)),
                pl.BlockSpec((SUB, lanes), lambda n, g, *_: (g, 0)),
                pl.BlockSpec((SUB, lanes), lambda n, g, *_: (g, 0)),
                pl.BlockSpec((1, 1, lanes), lambda n, g, *_: (n, 0, 0)),
            ],
            out_specs=pl.BlockSpec((1, SUB, tile, lanes), lambda n, g, *_: (n, g, 0, 0)),
            scratch_shapes=[pltpu.VMEM((tile * SUB, lanes), F32)],
        ),
        out_shape=jax.ShapeDtypeStruct((count, cols, tile, lanes), F32),
        compiler_params=params(2),
        cost_estimate=cost(0, count * cols * tile * lanes * 12),
        name="place_rows",
    )(rows0, rows1, where, first, second, cols0, cols1, diag[:, None, :])


def eliminate(block):
    tile = block.shape[0]
    lane = lax.broadcasted_iota(jnp.int32, (1, tile), 1)
    sub = lax.broadcasted_iota(jnp.int32, (tile, 1), 0)

    def at_lane(value, j):
        index = jnp.full(value.shape, j, jnp.int32)
        return jnp.take_along_axis(value, index, axis=1, mode="promise_in_bounds")

    def body(g, carry):
        at = pl.multiple_of(g * SUB, SUB)
        rows = block[pl.ds(at, SUB), :]
        whole = block[...].reshape(tile // SUB, SUB, tile)
        within = lax.broadcasted_iota(jnp.int32, (SUB, tile), 0)
        below = sub.reshape(tile // SUB, SUB, 1) >= at + SUB
        for r in range(SUB):
            j = at + r
            here = lane == j
            row = jnp.broadcast_to(rows[r : r + 1, :], (SUB, tile))
            pivot = at_lane(row, j)
            root = lax.rsqrt(pivot)
            root = root * (1.5 - 0.5 * pivot * root * root)
            row = jnp.where(here, root, row * root)
            column = at_lane(rows, j) * root
            under = within > r
            rows = jnp.where(
                under,
                jnp.where(here, 0.0, rows) - column * row,
                jnp.where(within == r, row, rows),
            )
            column = at_lane(whole.reshape(tile, tile), j).reshape(whole.shape) * root[None]
            whole = jnp.where(here[None], 0.0, whole) - column * row[None]
        block[...] = jnp.where(below, whole, block[...].reshape(whole.shape)).reshape(tile, tile)
        block[pl.ds(at, SUB), :] = rows
        return carry

    lax.fori_loop(0, tile // SUB, body, 0)
    low = lax.broadcasted_iota(jnp.int32, (tile, tile), 0) >= (
        lax.broadcasted_iota(jnp.int32, (tile, tile), 1)
    )
    return jnp.where(low, block[...], 0.0)


def inverse_factor(pivot, tile):
    order = pivot.shape[0]
    steps = order // tile

    def kernel(a, high, low, m, block):
        m[...] = a[...]
        for s in range(steps):
            top, end = s * tile, (s + 1) * tile
            block[...] = m[top:end, top:end]
            inverse = eliminate(block)
            strip = dot_full(inverse, m[top:end, :], ((1,), (0,)))
            pieces = [strip[:, :top]] if top > 0 else []
            pieces += [inverse] + ([strip[:, end:]] if end < order else [])
            strip = jnp.concatenate(pieces, axis=1)
            if end < order:
                m[end:, top:end] = jnp.zeros((order - end, tile), F32)
                m[end:, :] -= dot_full(strip[:, end:], strip, ((0,), (0,)))
                m[top:end, end:] = jnp.zeros((tile, order - end), F32)
            m[top:end, :end] = strip[:, :end]
        head, tail = split(m[...])
        high[...] = head
        low[...] = tail

    return pl.pallas_call(
        kernel,
        in_specs=[pl.BlockSpec(memory_space=pltpu.VMEM)],
        out_specs=[pl.BlockSpec(memory_space=pltpu.VMEM)] * 2,
        out_shape=[jax.ShapeDtypeStruct((order, order), BF16)] * 2,
        scratch_shapes=[pltpu.VMEM((order, order), F32), pltpu.VMEM((tile, tile), F32)],
        compiler_params=pltpu.CompilerParams(vmem_limit_bytes=VMEM_LIMIT),
        cost_estimate=cost(100e9, order * order * 8),
        name="inverse_factor",
    )(pivot)


def solve_rows(gathered, high, low, column_index):
    columns, rows, local = gathered.shape
    order = high.shape[0]
    tile = 128
    pieces = local // tile
    step = 256

    def kernel(me, f, h, l, out_h, out_l, out_f, acc):
        total = jnp.zeros((step, order), F32)
        for c in range(columns):
            fh, fl = split(f[c])
            spans = [
                slice((n * columns + c) * tile, (n * columns + c + 1) * tile) for n in range(pieces)
            ]
            gh = jnp.concatenate([h[:, s] for s in spans], axis=1)
            gl = jnp.concatenate([l[:, s] for s in spans], axis=1)
            total += dot_nt(fh, gh) + (dot_nt(fh, gl) + dot_nt(fl, gh))
        acc[...] = total
        xh, xl = split(total)
        out_h[...] = xh
        out_l[...] = xl
        for n in range(pieces):
            at = pl.multiple_of((n * columns + me[0]) * tile, tile)
            out_f[n] = acc[:, pl.ds(at, tile)]

    return pl.pallas_call(
        kernel,
        grid_spec=pltpu.PrefetchScalarGridSpec(
            num_scalar_prefetch=1,
            grid=(rows // step,),
            in_specs=[
                pl.BlockSpec((columns, step, local), lambda r, *_: (0, r, 0)),
                pl.BlockSpec((order, order), lambda r, *_: (0, 0)),
                pl.BlockSpec((order, order), lambda r, *_: (0, 0)),
            ],
            out_specs=[
                pl.BlockSpec((step, order), lambda r, *_: (r, 0)),
                pl.BlockSpec((step, order), lambda r, *_: (r, 0)),
                pl.BlockSpec((pieces, step, tile), lambda r, *_: (0, r, 0)),
            ],
            scratch_shapes=[pltpu.VMEM((step, order), F32)],
        ),
        out_shape=[
            jax.ShapeDtypeStruct((rows, order), BF16),
            jax.ShapeDtypeStruct((rows, order), BF16),
            jax.ShapeDtypeStruct((pieces, rows, tile), F32),
        ],
        compiler_params=params(),
        cost_estimate=cost(6 * rows * order * order, rows * order * 8),
        name="solve_rows",
    )(column_index, gathered, high, low)


def solve_columns(parts, homes, high, low):
    _, cols, tile, lanes = parts[0].shape
    order = high.shape[0]
    wide = 4
    deep = 256
    width = len(parts)

    def kernel(home, *refs):
        f, (h, l, out_h, out_l, fh, fl) = refs[:width], refs[width:]
        number = 0
        for part in f:
            for b in range(part.shape[0]):
                block = jnp.concatenate([part[b, p] for p in range(wide)], axis=1)
                rows = pl.ds(pl.multiple_of(home[number] * tile, tile), tile)
                fh[rows, :], fl[rows, :] = split(block)
                number += 1
        for r in range(order // deep):
            span, depth = slice(r * deep, (r + 1) * deep), (r + 1) * deep
            lh, ll = h[span, :depth], l[span, :depth]
            x = dot(lh, fh[:depth]) + (dot(lh, fl[:depth]) + dot(ll, fh[:depth]))
            out_h[span, :], out_l[span, :] = split(x)

    return pl.pallas_call(
        kernel,
        grid_spec=pltpu.PrefetchScalarGridSpec(
            num_scalar_prefetch=1,
            grid=(cols // wide,),
            in_specs=[
                pl.BlockSpec((part.shape[0], wide, tile, lanes), lambda g, *_: (0, g, 0, 0))
                for part in parts
            ]
            + [pl.BlockSpec((order, order), lambda g, *_: (0, 0))] * 2,
            out_specs=[pl.BlockSpec((order, wide * lanes), lambda g, *_: (0, g))] * 2,
            scratch_shapes=[pltpu.VMEM((order, wide * lanes), BF16)] * 2,
        ),
        out_shape=[jax.ShapeDtypeStruct((order, cols * lanes), BF16)] * 2,
        compiler_params=params(),
        cost_estimate=cost(4 * order * order * cols * lanes, order * cols * lanes * 8),
        name="solve_columns",
    )(homes, *parts, high, low)


def own_part(before, child, half, own_maps, diag, where, left, right, panel, start, end):
    _, _, rows, tile, cols, lanes = child.shape
    rowmap, colmap = own_maps
    xh, xl = left
    ch, cl = right
    order = xh.shape[1]
    count = panel.shape[0]
    block = min(4, rows)

    def kernel(half_ref, map_ref, where_ref, *refs):
        u, c, d, lh, ll, rh, rl, pan, out, flat = refs[-10:]
        g, n = pl.program_id(0) + start, pl.program_id(1)
        columns = c[...]
        for b in range(block):
            j = n * block + b

            def put(at, values):
                for r, value in enumerate(values):
                    spot = pl.multiple_of((b * tile + at + r) * SUB, SUB)
                    flat[pl.ds(spot, SUB), :] = value

            place_block(map_ref, j, lambda s: u[0, 0, b, s], columns, put)
            for p in range(SUB):
                @pl.when(where_ref[j] == g * SUB + p)
                def _():
                    eye = lax.broadcasted_iota(jnp.int32, (tile, lanes), 0) == (
                        lax.broadcasted_iota(jnp.int32, (tile, lanes), 1)
                    )
                    flat[pl.ds(b * tile * SUB + p, tile, SUB), :] += jnp.where(eye, d[b], 0.0)
        lhs_h, lhs_l = lh[...], ll[...]
        for pair in range(SUB // 2):
            span = slice(pair * 2 * lanes, (pair + 1) * 2 * lanes)
            update = dot(lhs_h, rh[:, span]) + (dot(lhs_h, rl[:, span]) + dot(lhs_l, rh[:, span]))
            for b in range(block):
                for side in range(2):
                    at = pl.ds(b * tile * SUB + 2 * pair + side, tile, SUB)
                    part = update[b * tile : (b + 1) * tile, side * lanes : (side + 1) * lanes]
                    flat[at, :] -= part

        @pl.when(g == 0)
        def _():
            for b in range(block):
                for p in range(count):
                    flat[pl.ds(b * tile * SUB + p, tile, SUB), :] = pan[
                        p, b * tile : (b + 1) * tile, :
                    ]

        out[...] = flat[...].reshape(out.shape)

    held = [] if before is None else [pl.BlockSpec(memory_space=pl.ANY)]
    return pl.pallas_call(
        kernel,
        grid_spec=pltpu.PrefetchScalarGridSpec(
            num_scalar_prefetch=3,
            grid=(end - start, rows // block),
            in_specs=held
            + [
                pl.BlockSpec(
                    (1, 1, block, tile, SUB, lanes), lambda g, n, h, *_: (0, h[0], n, 0, g + start, 0)
                ),
                pl.BlockSpec((SUB, lanes), lambda g, n, *_: (g + start, 0)),
                pl.BlockSpec((block, 1, lanes), lambda g, n, *_: (n, 0, 0)),
                pl.BlockSpec((block * tile, order), lambda g, n, *_: (n, 0)),
                pl.BlockSpec((block * tile, order), lambda g, n, *_: (n, 0)),
                pl.BlockSpec((order, SUB * lanes), lambda g, n, *_: (0, g + start)),
                pl.BlockSpec((order, SUB * lanes), lambda g, n, *_: (0, g + start)),
                pl.BlockSpec((count, block * tile, lanes), lambda g, n, *_: (0, n, 0)),
            ],
            out_specs=pl.BlockSpec((1, block, tile, SUB, lanes), lambda g, n, *_: (0, n, 0, g + start, 0)),
            scratch_shapes=[pltpu.VMEM((block * tile * SUB, lanes), F32)],
        ),
        out_shape=jax.ShapeDtypeStruct((1, rows, tile, cols, lanes), F32),
        input_output_aliases={} if before is None else {3: 0},
        compiler_params=params(2),
        cost_estimate=cost(
            6 * rows * tile * order * cols * lanes, rows * tile * cols * lanes * 8
        ),
        name="own_part",
    )(half, rowmap, where, *([] if before is None else [before]), child, colmap, diag[:, None, :], xh, xl, ch, cl, panel)


def add_first(front, block, rowmap, colmap):
    _, _, tile, cols, lanes = front.shape

    def kernel(map_ref, before, u, c, out):
        def add(at, values):
            values = [before[0, 0, at + r] + value for r, value in enumerate(values)]
            for r, value in enumerate(values):
                out[0, 0, at + r] = value

        place_block(map_ref, 0, lambda s: u[0, s], c[...], add)

    spec = pl.BlockSpec((1, 1, tile, SUB, lanes), lambda g, *_: (0, 0, 0, g, 0))
    return pl.pallas_call(
        kernel,
        grid_spec=pltpu.PrefetchScalarGridSpec(
            num_scalar_prefetch=1,
            grid=(cols // SUB,),
            in_specs=[
                spec,
                pl.BlockSpec((1, tile, SUB, lanes), lambda g, *_: (0, 0, g, 0)),
                pl.BlockSpec((SUB, lanes), lambda g, *_: (g, 0)),
            ],
            out_specs=spec,
        ),
        out_shape=jax.ShapeDtypeStruct(front.shape, F32),
        input_output_aliases={1: 0},
        compiler_params=params(),
        cost_estimate=cost(0, tile * cols * lanes * 12),
        name="add_first",
    )(rowmap, front, block, colmap)


def add_tiles(front, entries, steps, rowmap, colmap):
    _, _, tile, cols, lanes = front.shape
    sources, picks, stands = [], [], []
    for array, pick, stand, ever in entries:
        for slot in range(len(ever)):
            if ever[slot]:
                sources.append(array)
                picks.append(pick[slot])
                stands.append(stand[slot])
    width, count = len(sources), len(steps)
    picks, stands = (jnp.concatenate(t).astype(jnp.int32) for t in (picks, stands))
    order = jnp.array([row for row, _ in steps] + [group for _, group in steps], jnp.int32)

    def kernel(map_ref, order_ref, picks_ref, stands_ref, before, *refs):
        tiles, (c, out, flat) = refs[:width], refs[width:]
        n = pl.program_id(0)
        sub = lax.broadcasted_iota(jnp.int32, (SUB, lanes), 0)
        given = jnp.zeros((SUB, lanes), jnp.int32)
        for slot in range(width):
            stand = stands_ref[slot * count + n]
            p = stand // 2
            given = jnp.where((stand >= 0) & (sub == p), 1, given)

            @pl.when((stand >= 0) & (stand % 2 == 0))
            def _():
                flat[pl.ds(p, tile, SUB), :] = tiles[slot][0]

            @pl.when((stand >= 0) & (stand % 2 == 1))
            def _():
                flat[pl.ds(p, tile, SUB), :] = tiles[slot][0].T

        def load(source):
            return flat[pl.ds(pl.multiple_of(source * SUB, SUB), SUB), :]

        def add(at, values):
            values = [before[0, 0, at + r] + value for r, value in enumerate(values)]
            for r, value in enumerate(values):
                out[0, 0, at + r] = value

        place_block(map_ref, order_ref[n], load, jnp.where(given == 1, c[...], -1), add)

    spec = pl.BlockSpec(
        (1, 1, tile, SUB, lanes), lambda n, m, o, *_: (0, o[n], 0, o[count + n], 0)
    )

    def tile_spec(slot):
        return pl.BlockSpec((1, tile, lanes), lambda n, m, o, k, t: (k[slot * count + n], 0, 0))

    return pl.pallas_call(
        kernel,
        grid_spec=pltpu.PrefetchScalarGridSpec(
            num_scalar_prefetch=4,
            grid=(count,),
            in_specs=[spec]
            + [tile_spec(slot) for slot in range(width)]
            + [pl.BlockSpec((SUB, lanes), lambda n, m, o, *_: (o[count + n], 0))],
            out_specs=spec,
            scratch_shapes=[pltpu.VMEM((tile * SUB, lanes), F32)],
        ),
        out_shape=jax.ShapeDtypeStruct(front.shape, F32),
        input_output_aliases={4: 0},
        compiler_params=params(),
        cost_estimate=cost(0, count * tile * SUB * lanes * 12),
        name="add_tiles",
    )(rowmap, order, picks, stands, front, *sources, colmap)


def held_picks(picks, given):
    held = np.where(given, picks, 0)
    for step in range(1, held.shape[1]):
        held[:, step] = np.where(given[:, step], held[:, step], held[:, step - 1])
    return held.astype(np.int32)


def straight_entry(array, first, last, rows, parity, steps):
    j, g = np.array(steps).T
    i = g[None, :] * (SUB // 2) + np.arange(SUB // 2)[:, None]
    begins = np.array([lower_start(max(row, first), first, last) for row in range(rows)])
    given = (i >= first) & (i < last) & (i <= j)
    picks = held_picks(begins[j] + i - first, given)
    place = 2 * (2 * np.arange(SUB // 2)[:, None] + parity)
    return array, jnp.asarray(picks), jnp.where(given, place, -1), given.any(axis=1)


def turned_entry(array, first, last, rows, parity, steps, used):
    j, g = np.array(steps).T
    i = g[None, :] * (SUB // 2) + np.arange(SUB // 2)[:, None]
    begins = np.array([lower_start(max(row, first), first, last) for row in range(rows)])
    given = (j >= first) & (j < last) & (i > j)
    picks = held_picks(begins[i] + j - first, given)
    place = 2 * (2 * np.arange(SUB // 2)[:, None] + parity) + 1
    stands = jnp.where(given & used, place, -1)
    return array, jnp.where(used, picks, 0), stands, given.any(axis=1)


def cross_entry(array, rows, parity, steps):
    j, g = np.array(steps).T
    i = g[None, :] * (SUB // 2) + np.arange(SUB // 2)[:, None]
    given = i >= 1
    picks = held_picks((j - j[0]) * (rows - 1) + i - 1, given)
    place = 2 * (2 * np.arange(SUB // 2)[:, None] + parity)
    return array, jnp.asarray(picks), jnp.where(given, place, -1), given.any(axis=1)


def on_device(child_update, child_map, parent_diag):
    grid_size = lax.axis_size(("cube", "row"))
    half_grid = grid_size // 2
    columns = lax.axis_size("col")
    position = lax.axis_index(("cube", "row"))
    column_index = lax.axis_index("col")
    sibling = position // half_grid
    within = position % half_grid
    _, _, rows, tile, cols, lanes = child_update.shape
    distance = half_grid.bit_length() - 1
    pivots = K // tile
    local = pivots // columns
    mirrored = (
        grid_size == pivots
        and half_grid == columns
        and lax.axis_size("row") == half_grid
        and cols == 2 * rows
    )
    own = sibling.astype(jnp.int32)[None]
    other = 1 - own

    starts = tile * jnp.arange(rows * grid_size, dtype=jnp.int32)
    sources = jnp.stack(
        [inverse_map(child_map[e].reshape(-1, tile), starts) for e in range(2)]
    )

    def row_maps(child):
        of = lax.dynamic_index_in_dim(sources, child, 0, keepdims=False)
        of = of.reshape(rows, 2, half_grid, tile)
        return lax.dynamic_index_in_dim(of, within, 2, keepdims=False)

    def col_maps(child):
        of = lax.dynamic_index_in_dim(sources, child, 0, keepdims=False)
        of = of.reshape(cols, columns, tile)
        return lax.dynamic_index_in_dim(of, column_index, 1, keepdims=False)

    own_halves, other_halves = row_maps(sibling), row_maps(1 - sibling)
    own_cols, other_cols = col_maps(sibling), col_maps(1 - sibling)
    own_rows = lax.dynamic_index_in_dim(own_halves, sibling, 1, keepdims=False)
    other_rows = lax.dynamic_index_in_dim(other_halves, sibling, 1, keepdims=False)
    trailing_cols = jnp.where(jnp.arange(cols)[:, None] < local, -1, other_cols)

    blocks = grid_size * jnp.arange(rows, dtype=jnp.int32) + position
    diag_tiles = parent_diag.reshape(-1, tile)

    def on_diagonal(block_rows):
        offset = block_rows - column_index
        return jnp.where(offset % columns == 0, offset // columns, -1).astype(jnp.int32)

    diag_rows = diag_tiles[blocks]

    subcubes = ("cube", "row")
    spans, at = [], 1
    while at < rows:
        count = -(-3 * (rows - at) // 10)
        spans.append((at, count))
        at += count

    panel_sent = pack_panel(child_update, other, local)
    panel_own = pack_panel(after(child_update, panel_sent), own, local)
    panel_came = swapped(panel_sent, subcubes, distance)
    if mirrored:
        near = spans[0][0] + spans[0][1]
        edges = [1, 2, 4, near, near + 2, rows]
        cuts = list(zip(edges[:-1], edges[1:]))
        lower_sent = [pack_lower(child_update, other, other, a, b) for a, b in cuts]
        pivot_sent = after(child_update, panel_sent)[0, :, 0]
        panel_came = after(panel_came, panel_own, pivot_sent, *lower_sent[:3])
    else:
        pivot_sent = lax.dynamic_slice_in_dim(child_update[0, :, 0], 1 - sibling, 1, 0)

    def placed(tiles, row_map, col_map):
        offsets = jnp.arange(tile, dtype=jnp.int32)
        row_hot = (row_map[:, :, None] == offsets).astype(F32)
        col_hot = (col_map[:local, :, None] == offsets).astype(F32)
        done = jnp.einsum("jos,jpsv->jpov", row_hot, tiles, precision=lax.Precision.HIGHEST)
        return jnp.einsum("jpov,pqv->jopq", done, col_hot, precision=lax.Precision.HIGHEST)

    hits = on_diagonal(blocks)[:, None] == jnp.arange(local)
    eye = jnp.eye(tile, dtype=bool)[None, :, None, :] & hits[:, None, :, None]
    front_panel = placed(panel_own, own_rows, own_cols)
    front_panel += placed(panel_came, other_rows, other_cols)
    front_panel += jnp.where(eye, diag_rows[:, :, None, None], 0.0)

    pivot = lax.all_gather(front_panel[0], ("cube", "row", "col"), axis=0, tiled=False)
    gathered = lax.all_gather(
        front_panel.reshape(rows * tile, local * tile), "col", axis=0, tiled=False
    )
    pivot = pivot.reshape(grid_size, columns, tile, local, tile)[:pivots]
    pivot = jnp.transpose(pivot, (0, 2, 3, 1, 4)).reshape(K, K)

    pivot_came = swapped(pivot_sent, subcubes, distance)
    if mirrored:
        pairs = [
            (r * columns + c, c * columns + r)
            for r in range(half_grid)
            for c in range(columns)
            if r != c
        ]
        lower = [swapped(after(part, front_panel), subcubes, distance) for part in lower_sent[:3]]
        sent = pack_cross(after(child_update, front_panel), other, own)
        pivot_came = after(pivot_came, sent, *lower_sent[3:])
        lower += [swapped(after(part, pivot_came), subcubes, distance) for part in lower_sent[3:]]
        block_rows = half_grid * jnp.arange(2, dtype=jnp.int32) + within
        pivot_rows = place_rows(
            pivot_sent,
            pivot_came,
            ((own_halves[0], own_cols), (other_halves[0], other_cols)),
            diag_tiles[block_rows],
            on_diagonal(block_rows),
        )
        across = swapped(pivot_rows, "row", 1)
        pivot = after(pivot, pivot_rows)
    else:
        sent = pack_all(child_update, other)
    high, low = inverse_factor(pivot, tile)

    came = []

    def send(number, behind):
        at, count = spans[number]
        part = after(sent[at - 1 : at - 1 + count], behind)
        came.append(swapped(part, subcubes, distance))

    if mirrored:
        lower[:2] = [after(part, high) for part in lower[:2]]
        turned = [lax.ppermute(part, ("row", "col"), pairs) for part in lower[:2]]
        send(0, lower[1])
        gathered = after(gathered, *lower[:2])
    left_h, left_l, panel = solve_rows(gathered, high, low, column_index.astype(jnp.int32)[None])
    if mirrored:
        across = after(across, left_h, lower[2], lower[3])
        beside = swapped(jnp.concatenate([pivot_rows, across]), "row", 0)
        parts = [pivot_rows, across, beside]
        homes = [block_rows ^ bits for bits in (0, 2, 1, 3)]
        first = lax.dynamic_slice_in_dim(pivot_came, sibling, 1, 0)
    else:
        for number in range(len(spans)):
            send(number, came[-2] if number > 1 else pivot_came)
        pivot_rows = place_rows(
            lax.dynamic_slice_in_dim(child_update[0, :, 0], sibling, 1, 0),
            pivot_came,
            ((own_rows[:1], own_cols), (other_rows[:1], other_cols)),
            diag_rows[:1],
            on_diagonal(blocks[:1]),
        )
        mine = (jnp.arange(pivots) == position)[:, None, None, None]
        parts = [lax.psum(jnp.where(mine, pivot_rows, 0.0), subcubes)]
        homes = [jnp.arange(pivots, dtype=jnp.int32)]
        first = pivot_came
    right_h, right_l = solve_columns(parts, jnp.concatenate(homes), high, low)
    if mirrored:
        turned += [lax.ppermute(part, ("row", "col"), pairs) for part in lower[2:4]]

    front = None
    groups = cols // SUB
    for start, end in ((0, groups // 2), (groups // 2, groups)):
        front = own_part(
            front,
            child_update,
            own,
            (own_rows, own_cols),
            diag_rows,
            on_diagonal(blocks),
            (left_h, left_l),
            (right_h, right_l),
            panel,
            start,
            end,
        )
        if mirrored:
            if start == 0:
                turned[0] = after(turned[0], front)
                send(1, turned[0])
                front = after(front, turned[0])
            else:
                send(2, front)
                lower[4] = after(lower[4], front)
                front = after(front, turned[2], lower[4])
    front = add_first(front, first, other_rows[:1], trailing_cols)

    def turned_tiles(front, parts, low, top):
        steps = [
            (j, g)
            for j in range(low, top)
            for g in range(groups)
            if j < min(rows, (g + 1) * (SUB // 2)) - 1
        ]
        alone = within == column_index
        entries = []
        for part in parts:
            mine = (*cuts[part], rows, sibling, steps)
            entries.append(turned_entry(turned[part], *mine, ~alone))
            entries.append(turned_entry(lower[part], *mine, alone))
        return add_tiles(front, entries, steps, other_rows, trailing_cols)

    for number, (at, count) in enumerate(spans):
        if len(came) < len(spans):
            send(len(came), front)
        flat = came[number].reshape(-1, tile, tile)
        steps = [(j, g) for j in range(at, at + count) for g in range(groups)]
        if mirrored:
            if number == 1:
                turned.append(lax.ppermute(after(lower[4], front), ("row", "col"), pairs))
                front = after(front, turned[1])
            if number == 2:
                front = turned_tiles(after(front, turned[3]), (0, 1, 2), 1, near)
            if number == len(spans) - 1:
                front = turned_tiles(front, (3, 4), near, rows)
            entries = [cross_entry(flat, rows, 1 - sibling, steps)]
            for part, cut in zip(lower, cuts):
                entries.append(straight_entry(part, *cut, rows, sibling, steps))
        else:
            j, g = np.array(steps).T
            slot = np.arange(SUB)[:, None]
            picks = jnp.asarray((j - at) * cols + g * SUB + slot, jnp.int32)
            stands = jnp.asarray(np.broadcast_to(2 * slot, picks.shape), jnp.int32)
            entries = [(flat, picks, stands, np.ones(SUB, bool))]
        front = add_tiles(front, entries, steps, other_rows, trailing_cols)
    return front


def solution(mesh):
    return jax.shard_map(
        on_device,
        mesh=mesh,
        in_specs=(P(("cube", "row"), None, None, None, "col", None), P(), P()),
        out_specs=P(("cube", "row"), None, None, "col", None),
        check_vma=False,
    )
```
